32 devices in a mesh: gx: 8 (over z, core), gy: 4 (over y, x).
Axes of the slice: x: 2, y: 2, z: 4, core: 2. Of those that a mesh axis runs over, the one named last changes fastest.
Arguments:
- rhs_leaf: float32 [8, 4, 8, 512], P('gx', 'gy'), may hold values from -6 to 6
- leaf_inv: float32 [8, 4, 4, 128, 128], P('gx', 'gy'), may hold values from -0.5 to 0.5
- leaf_sub: float32 [8, 4, 3, 128, 128], P('gx', 'gy'), may hold values from -0.375 to 0.375
- sep_rhs: float32 [8, 4, 8, 96], P('gx', 'gy'), may hold values from -6 to 6
- interface: int32 [8, 4, 4, 128], P('gx', 'gy'), may hold values from 0 to 511, as said below
- coupling: float32 [8, 4, 4, 128, 512], P('gx', 'gy'), may hold values from -0.125 to 0.125
- factor_one: float32 [8, 4, 16, 512], P('gx', 'gy'), may hold values from -0.25 to 0.25
- factor_two: float32 [8, 4, 16, 256], P('gx', 'gy'), may hold values from -0.375 to 0.375
- factor_three: float32 [8, 4, 32, 256], P('gx', 'gy'), may hold values from -0.375 to 0.375
- factor_four: float32 [8, 4, 32, 128], P('gx', 'gy'), may hold values from -0.5 to 0.5
- link_two: float32 [8, 4, 16, 128], P('gx', 'gy'), may hold values from -0.375 to 0.375
- link_three: float32 [8, 4, 32, 128], P('gx', 'gy'), may hold values from -0.25 to 0.25
- link_four: float32 [8, 4, 32, 128], P('gx', 'gy'), may hold values from -0.25 to 0.25
Outputs:
- leaf_solution: float32 [8, 4, 8, 512], P('gx', 'gy')
- sep_solution: float32 [8, 4, 8, 96], P('gx', 'gy')
The draws below stay inside these ranges and needn't reach their ends.
Inputs may be any that keep to these rules, and one draw needn't show every extreme that they name: interface[a, c, k-1, n] is a position of a level-k separator, below S_k, and S_k - 1 is reached at every level; positions may repeat within a leaf.
All inputs are finite; a program needn't handle non-finite values.
Results may differ from the reference program's by a relative error of at most 0.00014.
Values sent between devices are 32-bit elements; how exact they have to be, the bound alone decides.
No kernel may reach another device: no remote copies, remote signals or barrier semaphores. Data moves between devices by JAX's collectives and lax.ppermute only.
A program may use at most 64 MiB of HBM per device.

```python
import jax
import jax.numpy as jnp
import numpy as np
from jax import lax

R = 8
BL = 128
NB = 4
NIF = 128
SROWS = 16
NL = 512
BLOCKS_X = 8
BLOCKS_Y = 4
SEP1 = 512
SEP2 = 256
SEP3 = 256
SEP4 = 128
ALLROWS = 96
N_GX = 8
N_GY = 4


def draw_interface(key, part):
    tops = [SEP1, SEP2, SEP3, SEP4]
    columns = []
    for section in range(4):
        values = jax.random.randint(jax.random.fold_in(key, 101 + section), (BLOCKS_X, BLOCKS_Y, NIF), 0, tops[section], dtype=jnp.int32)
        values = values.at[0, 0, 0].set(tops[section] - 1)
        values = values.at[0, 0, 1].set(0)
        columns.append(values)
    return jnp.stack(columns, axis=2)


def block_scale(own_key, extent, cuts, smallest, largest):
    loudness = 1.0
    for axis_at, shards_of in cuts:
        steps = jax.random.uniform(jax.random.fold_in(jax.random.fold_in(own_key, 6), axis_at), (shards_of,), jnp.float32, smallest / len(cuts), largest / len(cuts))
        loudness = loudness * jnp.repeat(jnp.exp(steps), extent[axis_at] // shards_of).reshape((-1,) + (1,) * (len(extent) - 1 - axis_at))
    return loudness


def normal_values(rng, dims, width, reach, split=(), kind=jnp.bfloat16):
    loudness = block_scale(rng, dims, split, -0.22, 0.18) if split else 1.0
    drawn = jax.random.normal(rng, dims, jnp.float32) * width * loudness
    return jnp.minimum(jnp.maximum(drawn, -reach), reach).astype(kind)


def setup_inputs(seed: int = 0) -> dict:
    arg_keys = jax.random.split(jax.random.key(seed), 14)
    rhs_leaf = normal_values(arg_keys[0], (BLOCKS_X, BLOCKS_Y, R, NL), 1.0, 6.0, ((0, 8), (1, 4)), jnp.float32)
    leaf_inv = normal_values(arg_keys[1], (BLOCKS_X, BLOCKS_Y, NB, BL, BL), BL ** -0.5, 0.5, ((0, 8), (1, 4)), jnp.float32)
    leaf_sub = normal_values(arg_keys[2], (BLOCKS_X, BLOCKS_Y, NB - 1, BL, BL), (2 * BL) ** -0.5, 0.375, ((0, 8), (1, 4)), jnp.float32)
    sep_rhs = normal_values(arg_keys[3], (BLOCKS_X, BLOCKS_Y, R, ALLROWS), 1.0, 6.0, ((0, 8), (1, 4)), jnp.float32)
    interface = draw_interface(jax.random.fold_in(arg_keys[13], 71), 0)
    coupling = normal_values(arg_keys[5], (BLOCKS_X, BLOCKS_Y, 4, NIF, NL), (4 * NL) ** -0.5, 0.125, ((0, 8), (1, 4)), jnp.float32)
    factor_one = normal_values(arg_keys[6], (BLOCKS_X, BLOCKS_Y, SROWS, SEP1), SEP1 ** -0.5, 0.25, ((0, 8), (1, 4)), jnp.float32)
    factor_two = normal_values(arg_keys[7], (BLOCKS_X, BLOCKS_Y, SROWS, SEP2), SEP2 ** -0.5, 0.375, ((0, 8), (1, 4)), jnp.float32)
    factor_three = normal_values(arg_keys[8], (BLOCKS_X, BLOCKS_Y, 2 * SROWS, SEP3), SEP3 ** -0.5, 0.375, ((0, 8), (1, 4)), jnp.float32)
    factor_four = normal_values(arg_keys[9], (BLOCKS_X, BLOCKS_Y, 2 * SROWS, SEP4), SEP4 ** -0.5, 0.5, ((0, 8), (1, 4)), jnp.float32)
    link_two = normal_values(arg_keys[10], (BLOCKS_X, BLOCKS_Y, SROWS, NIF), (16 * SROWS) ** -0.5, 0.375, ((0, 8), (1, 4)), jnp.float32)
    link_three = normal_values(arg_keys[11], (BLOCKS_X, BLOCKS_Y, 2 * SROWS, NIF), (32 * SROWS) ** -0.5, 0.25, ((0, 8), (1, 4)), jnp.float32)
    link_four = normal_values(arg_keys[12], (BLOCKS_X, BLOCKS_Y, 2 * SROWS, NIF), (32 * SROWS) ** -0.5, 0.25, ((0, 8), (1, 4)), jnp.float32)
    return {"rhs_leaf": rhs_leaf, "leaf_inv": leaf_inv, "leaf_sub": leaf_sub, "sep_rhs": sep_rhs, "interface": interface, "coupling": coupling, "factor_one": factor_one, "factor_two": factor_two, "factor_three": factor_three, "factor_four": factor_four, "link_two": link_two, "link_three": link_three, "link_four": link_four}


PRECISE = lax.Precision.HIGHEST


def taken_lists():
    gy_bits = N_GY.bit_length() - 1
    gx_bits = N_GX.bit_length() - 1
    first = list(range(gy_bits + gx_bits))
    second = [bit_number for bit_number in first if bit_number != gy_bits + gx_bits - 1]
    third = [bit_number for bit_number in second if bit_number != gy_bits - 1]
    fourth = [bit_number for bit_number in third if bit_number != gy_bits + gx_bits - 2]
    return [first, second, third, fourth]


def group_tables(taken):
    device_ids = np.arange(N_GX * N_GY)
    group_rank = device_ids * 0
    for bit_number in sorted(taken, reverse=True):
        group_rank = group_rank * 2 + ((device_ids >> bit_number) & 1)
    taken_mask = 0
    for bit_number in taken:
        taken_mask = taken_mask + (1 << bit_number)
    group_keys, group_of = np.unique(device_ids & (~taken_mask), return_inverse=True)
    return group_rank, group_of.reshape(-1), len(group_keys)


def leaf_forward(right_side, inverse_blocks, lower_blocks):
    results = []
    earlier = None
    for counter in range(NB):
        current = right_side[:, :, counter * BL:(counter + 1) * BL]
        if counter > 0:
            current = current - jnp.einsum('drk,dkl->drl', earlier, lower_blocks[:, counter - 1], precision=PRECISE)
        earlier = jnp.einsum('drk,dkl->drl', current, inverse_blocks[:, counter], precision=PRECISE)
        results.append(earlier)
    return jnp.concatenate(results, axis=2)


def leaf_backward(leaf_work, inverse_blocks, lower_blocks):
    results = [None] * NB
    later = None
    for counter in reversed(range(NB)):
        current = leaf_work[:, :, counter * BL:(counter + 1) * BL]
        if counter < NB - 1:
            current = current - jnp.einsum('drl,dkl->drk', later, lower_blocks[:, counter], precision=PRECISE)
        later = jnp.einsum('drl,dkl->drk', current, inverse_blocks[:, counter], precision=PRECISE)
        results[counter] = later
    return jnp.concatenate(results, axis=2)


def reference(rhs_leaf, leaf_inv, leaf_sub, sep_rhs, interface, coupling, factor_one, factor_two, factor_three, factor_four, link_two, link_three, link_four):
    devices = N_GX * N_GY

    def flatten(array):
        return array.reshape((devices,) + array.shape[2:])

    factors = [flatten(factor_one), flatten(factor_two), flatten(factor_three), flatten(factor_four)]
    link_mats = [flatten(link_two), flatten(link_three), flatten(link_four)]
    places = flatten(interface)
    couplings = flatten(coupling)
    own_rhs = flatten(sep_rhs)
    inverse_blocks = flatten(leaf_inv)
    lower_blocks = flatten(leaf_sub)
    row_counts = [SROWS, SROWS, 2 * SROWS, 2 * SROWS]
    sep_widths = [SEP1, SEP2, SEP3, SEP4]
    offsets = [0, SROWS, 2 * SROWS, 4 * SROWS]
    group_index = []
    owned = []
    group_counts = []
    for taken in taken_lists():
        group_rank, group_of, group_count = group_tables(taken)
        group_index.append(jnp.asarray(group_of, dtype=jnp.int32)[:, None])
        own_rows = row_counts[len(owned)]
        owned.append(jnp.asarray(group_rank[:, None] * own_rows + np.arange(own_rows)[None, :], dtype=jnp.int32))
        group_counts.append(group_count)
    forward = leaf_forward(flatten(rhs_leaf), inverse_blocks, lower_blocks)
    own_z = [None] * 4
    for section in (3, 2, 1, 0):
        own_rows = row_counts[section]
        partials_in = jnp.einsum('drl,dnl->drn', forward, couplings[:, section], precision=PRECISE)
        if section < 3:
            partials_in = partials_in + jnp.einsum('drq,dqn->drn', own_z[section + 1], link_mats[section], precision=PRECISE)
        summed = jnp.zeros((group_counts[section], R, sep_widths[section]), jnp.float32)
        own_part = own_rhs[:, :, offsets[section]:offsets[section] + own_rows]
        summed = summed.at[group_index[section], :, owned[section]].add(jnp.transpose(own_part, (0, 2, 1)))
        summed = summed.at[group_index[section], :, places[:, section]].add(-jnp.transpose(partials_in, (0, 2, 1)))
        own_z[section] = jnp.einsum('drs,dqs->drq', summed[group_index[section][:, 0]], factors[section], precision=PRECISE)
    full_sep = [None] * 4
    own_x = []
    for section in range(4):
        update = own_z[section]
        if section > 0:
            picked = full_sep[section - 1][group_index[section - 1], :, places[:, section - 1]]
            update = update - jnp.einsum('dnr,dqn->drq', picked, link_mats[section - 1], precision=PRECISE)
        partial_value = jnp.einsum('drq,dqs->drs', update, factors[section], precision=PRECISE)
        full_sep[section] = jax.ops.segment_sum(partial_value, group_index[section][:, 0], num_segments=group_counts[section])
        own_x.append(jnp.transpose(full_sep[section][group_index[section], :, owned[section]], (0, 2, 1)))
    leaf_work = forward
    for section in range(4):
        picked = full_sep[section][group_index[section], :, places[:, section]]
        leaf_work = leaf_work - jnp.einsum('dnr,dnl->drl', picked, couplings[:, section], precision=PRECISE)
    leaf_solution = leaf_backward(leaf_work, inverse_blocks, lower_blocks)
    sep_solution = jnp.concatenate(own_x, axis=2)
    return leaf_solution.reshape(N_GX, N_GY, R, NL), sep_solution.reshape(N_GX, N_GY, R, 6 * SROWS)
```

```python
import functools

import jax
import jax.numpy as jnp
from jax import lax
from jax.experimental import pallas as pl
from jax.experimental.pallas import tpu as pltpu
from jax.sharding import PartitionSpec as P

PRECISE = lax.Precision.HIGHEST
LANES = 128
GATHER_BYTES = 8 * 2**20
VMEM_BYTES = 24 * 2**20


def from_partner(value, axis, distance):
    return lax.ppermute(value, axis, [(i, i ^ 1 << distance) for i in range(lax.axis_size(axis))])


def taken_lists(gy_bits, gx_bits):
    first = list(range(gy_bits + gx_bits))
    second = [bit_number for bit_number in first if bit_number != gy_bits + gx_bits - 1]
    third = [bit_number for bit_number in second if bit_number != gy_bits - 1]
    fourth = [bit_number for bit_number in third if bit_number != gy_bits + gx_bits - 2]
    return [first, second, third, fourth]


def rank_in_group(device_index, taken):
    group_rank = jnp.zeros((), jnp.int32)
    for bit_number in sorted(taken, reverse=True):
        group_rank = group_rank * 2 + (device_index >> bit_number & 1)
    return group_rank


def group_total(values, section, taken):
    if section == 0:
        return lax.psum(values, ("gx", "gy"))
    for bit_number in sorted(taken, reverse=True):
        values = values + from_partner(values, ("gx", "gy"), bit_number)
    return values


def leaf_forward(right_side, inverse_blocks, lower_blocks):
    block_size = inverse_blocks.shape[1]
    results = []
    earlier = None
    for counter in range(inverse_blocks.shape[0]):
        current = right_side[:, counter * block_size : (counter + 1) * block_size]
        if counter > 0:
            current = current - jnp.dot(earlier, lower_blocks[counter - 1], precision=PRECISE)
        earlier = jnp.dot(current, inverse_blocks[counter], precision=PRECISE)
        results.append(earlier)
    return jnp.concatenate(results, axis=1)


def leaf_backward(leaf_work, inverse_blocks, lower_blocks):
    block_size = inverse_blocks.shape[1]
    block_count = inverse_blocks.shape[0]
    contract_last = (((1,), (1,)), ((), ()))
    results = [None] * block_count
    later = None
    for counter in reversed(range(block_count)):
        current = leaf_work[:, counter * block_size : (counter + 1) * block_size]
        if counter < block_count - 1:
            current = current - lax.dot_general(
                later, lower_blocks[counter], contract_last, precision=PRECISE
            )
        later = lax.dot_general(current, inverse_blocks[counter], contract_last, precision=PRECISE)
        results[counter] = later
    return jnp.concatenate(results, axis=1)


def level_by_level(
    rhs_leaf,
    leaf_inv,
    leaf_sub,
    sep_rhs,
    interface,
    coupling,
    factor_one,
    factor_two,
    factor_three,
    factor_four,
    link_two,
    link_three,
    link_four,
):
    contract_last = (((1,), (1,)), ((), ()))
    gy_bits = lax.axis_size("gy").bit_length() - 1
    gx_bits = lax.axis_size("gx").bit_length() - 1
    sections = taken_lists(gy_bits, gx_bits)
    device_index = lax.axis_index(("gx", "gy"))
    factors = (factor_one[0, 0], factor_two[0, 0], factor_three[0, 0], factor_four[0, 0])
    link_mats = (link_two[0, 0], link_three[0, 0], link_four[0, 0])
    places = interface[0, 0]
    couplings = coupling[0, 0]
    own_rhs = sep_rhs[0, 0]
    inverse_blocks = leaf_inv[0, 0]
    lower_blocks = leaf_sub[0, 0]
    forward = leaf_forward(rhs_leaf[0, 0], inverse_blocks, lower_blocks)
    rhs_count = forward.shape[0]
    offsets = [0]
    for section in range(3):
        offsets.append(offsets[-1] + factors[section].shape[0])
    ranks = [rank_in_group(device_index, taken) for taken in sections]
    own_z = [None] * 4
    for section in (3, 2, 1, 0):
        own_rows, sep_width = factors[section].shape
        partials_in = lax.dot_general(forward, couplings[section], contract_last, precision=PRECISE)
        if section < 3:
            partials_in = partials_in + jnp.dot(
                own_z[section + 1], link_mats[section], precision=PRECISE
            )
        contribution = jnp.zeros((rhs_count, sep_width), jnp.float32)
        own_part = own_rhs[:, offsets[section] : offsets[section] + own_rows]
        contribution = lax.dynamic_update_slice(
            contribution, own_part, (jnp.zeros((), jnp.int32), ranks[section] * own_rows)
        )
        contribution = contribution.at[:, places[section]].add(-partials_in)
        summed = group_total(contribution, section, sections[section])
        own_z[section] = lax.dot_general(summed, factors[section], contract_last, precision=PRECISE)
    full_sep = [None] * 4
    own_x = []
    for section in range(4):
        own_rows = factors[section].shape[0]
        update = own_z[section]
        if section > 0:
            picked = full_sep[section - 1][:, places[section - 1]]
            update = update - lax.dot_general(
                picked, link_mats[section - 1], contract_last, precision=PRECISE
            )
        partial_value = jnp.dot(update, factors[section], precision=PRECISE)
        full_sep[section] = group_total(partial_value, section, sections[section])
        own_x.append(
            lax.dynamic_slice_in_dim(full_sep[section], ranks[section] * own_rows, own_rows, 1)
        )
    leaf_work = forward
    for section in range(4):
        picked = full_sep[section][:, places[section]]
        leaf_work = leaf_work - jnp.dot(picked, couplings[section], precision=PRECISE)
    leaf_solution = leaf_backward(leaf_work, inverse_blocks, lower_blocks)
    sep_solution = jnp.concatenate(own_x, axis=1)
    return (leaf_solution[None, None], sep_solution[None, None])


def halves(value):
    high = value.astype(jnp.bfloat16)
    low = (value - high.astype(jnp.float32)).astype(jnp.bfloat16)
    return high, low


def few_rows(value):
    high = value.astype(jnp.bfloat16).astype(jnp.float32)
    return jnp.concatenate([high, value - high], axis=0).astype(jnp.bfloat16)


def times(left, right, transposed):
    dims = (((1,), (1 if transposed else 0,)), ((), ()))
    stacked = few_rows(left)
    total = None
    for piece in right:
        term = lax.dot_general(stacked, piece, dims, preferred_element_type=jnp.float32)
        total = term if total is None else total + term
    rows = left.shape[0]
    return total[:rows] + total[rows:]


def one_hot(positions, height):
    rows = lax.broadcasted_iota(jnp.int32, (height, positions.shape[1]), 0)
    return (rows == positions).astype(jnp.float32).astype(jnp.bfloat16)


def wide(ref, start, rows, chunks):
    pieces = [ref[start + chunk * rows : start + (chunk + 1) * rows, :] for chunk in range(chunks)]
    return pieces[0] if chunks == 1 else jnp.concatenate(pieces, axis=1)


def vmem_call(body, outs, *operands):
    out_shape = [jax.ShapeDtypeStruct(shape, dtype) for shape, dtype in outs]
    return pl.pallas_call(
        body,
        out_shape=out_shape,
        in_specs=[pl.BlockSpec(memory_space=pltpu.VMEM)] * len(operands),
        out_specs=[pl.BlockSpec(memory_space=pltpu.VMEM)] * len(outs),
        compiler_params=pltpu.CompilerParams(vmem_limit_bytes=VMEM_BYTES),
    )(*operands)


def packed_layout(factors, link_mats):
    starts = {}
    at = 0
    for name, rows in (
        ("f0", factors[0].shape[0] * (factors[0].shape[1] // LANES)),
        ("f1", factors[1].shape[0] * (factors[1].shape[1] // LANES)),
        ("l1", link_mats[0].shape[0]),
        ("places", 8),
        ("f2", factors[2].shape[0] * (factors[2].shape[1] // LANES)),
        ("l2", link_mats[1].shape[0]),
        ("f3", factors[3].shape[0] * (factors[3].shape[1] // LANES)),
        ("l3", link_mats[2].shape[0]),
    ):
        starts[name] = at
        at += rows
    return starts, at


def pack_body(starts, f0, f1, f2, f3, l1, l2, l3, places, out):
    for name, ref in (("f0", f0), ("f1", f1), ("f2", f2), ("f3", f3)):
        rows, width = ref.shape[2:]
        for chunk in range(width // LANES):
            at = starts[name] + chunk * rows
            out[at : at + rows, :] = ref[0, 0, :, chunk * LANES : (chunk + 1) * LANES]
    for name, ref in (("l1", l1), ("l2", l2), ("l3", l3)):
        out[starts[name] : starts[name] + ref.shape[2], :] = ref[0, 0]
    numbers = places[0, 0].astype(jnp.float32)
    out[starts["places"] : starts["places"] + 8, :] = jnp.concatenate([numbers, numbers], axis=0)


def own_targets(sizes, owned, taken):
    device_index = lax.axis_index("gx") * lax.axis_size("gy") + lax.axis_index("gy")
    columns = lax.broadcasted_iota(jnp.int32, (1, sum(owned)), 1)
    target = columns
    before = 0
    level_start = 0
    for section in range(4):
        rank = jnp.int32(0)
        for bit_number in sorted(taken[section], reverse=True):
            rank = rank * 2 + ((device_index >> bit_number) & 1)
        here = columns - before + (level_start + rank * owned[section])
        target = jnp.where(columns >= before, here, target)
        before += owned[section]
        level_start += sizes[section]
    return target


def forward_body(sizes, owned, taken, rhs, inverse, lower, sep_rhs, places, coupling, forward, sums):
    count, block = inverse.shape[2], inverse.shape[3]
    earlier = None
    for counter in range(count):
        current = rhs[0, 0, :, counter * block : (counter + 1) * block]
        if counter > 0:
            current = current - times(earlier, halves(lower[0, 0, counter - 1]), False)
        earlier = times(current, halves(inverse[0, 0, counter]), False)
        forward[:, counter * block : (counter + 1) * block] = earlier
    whole = forward[...]
    own = times(sep_rhs[0, 0], [one_hot(own_targets(sizes, owned, taken), sum(sizes))], True)
    at = 0
    for section in range(4):
        term = times(whole, halves(coupling[0, 0, section]), True)
        spread = times(term, [one_hot(places[0, 0, section : section + 1, :], sizes[section])], True)
        sums[:, at : at + sizes[section]] = own[:, at : at + sizes[section]] - spread
        at += sizes[section]


def gather_body(section, starts, rows, size, above, strides, *refs):
    outs = refs[len(strides) :]
    at = 0
    for ref, (members, stride) in zip(refs, strides):
        for member in range(members):
            base = member * stride
            factor = wide(ref, base + starts["f%d" % section], rows, size // LANES)
            outs[0][at : at + rows, :], outs[1][at : at + rows, :] = halves(factor)
            if section > 0:
                begin = base + starts["l%d" % section]
                link = ref[begin : begin + rows, :]
                row = base + starts["places"] + section - 1
                positions = ref[row : row + 1, :].astype(jnp.int32)
                linked = times(link, [one_hot(positions, above)], True)
                outs[2][at : at + rows, :], outs[3][at : at + rows, :] = halves(linked)
            at += rows


def eliminate_body(size, above, mine, theirs, f_high, f_low, m_high, m_low, sums, found):
    width = mine.shape[1]
    total = mine[...] + theirs[...]
    solved = times(total[:, width - size :], [f_high[...], f_low[...]], True)
    found[...] = solved
    sums[:, : width - size] = total[:, : width - size]
    rest = total[:, width - size - above : width - size]
    sums[:, width - size - above :] = rest - times(solved, [m_high[...], m_low[...]], False)


def top_body(mine, theirs, f_high, f_low, partial):
    total = mine[...] + theirs[...]
    pieces = [f_high[...], f_low[...]]
    partial[...] = times(times(total, pieces, True), pieces, False)


def backward_body(
    sizes, owned, taken, mine, theirs, z1, z2, z3,
    f1h, f1l, m1h, m1l, f2h, f2l, m2h, m2l, f3h, f3l, m3h, m3l,
    forward, coupling, places, inverse, lower, leaf, sep,
):
    solved = [mine[...] + theirs[...]]
    levels = (
        (z1, f1h, f1l, m1h, m1l),
        (z2, f2h, f2l, m2h, m2l),
        (z3, f3h, f3l, m3h, m3l),
    )
    for found, f_high, f_low, m_high, m_low in levels:
        update = found[...] - times(solved[-1], [m_high[...], m_low[...]], True)
        solved.append(times(update, [f_high[...], f_low[...]], False))
    everything = jnp.concatenate(solved, axis=1)
    sep[0, 0] = times(everything, [one_hot(own_targets(sizes, owned, taken), sum(sizes))], False)
    work = forward[...]
    for section in range(4):
        picked = times(solved[section], [one_hot(places[0, 0, section : section + 1, :], sizes[section])], False)
        work = work - times(picked, halves(coupling[0, 0, section]), False)
    count, block = inverse.shape[2], inverse.shape[3]
    later = None
    for counter in reversed(range(count)):
        current = work[:, counter * block : (counter + 1) * block]
        if counter < count - 1:
            current = current - times(later, halves(lower[0, 0, counter]), True)
        later = times(current, halves(inverse[0, 0, counter]), True)
        leaf[0, 0, :, counter * block : (counter + 1) * block] = later


def gathered(
    rhs_leaf,
    leaf_inv,
    leaf_sub,
    sep_rhs,
    interface,
    coupling,
    factor_one,
    factor_two,
    factor_three,
    factor_four,
    link_two,
    link_three,
    link_four,
):
    gy_bits = lax.axis_size("gy").bit_length() - 1
    gx_bits = lax.axis_size("gx").bit_length() - 1
    taken = taken_lists(gy_bits, gx_bits)
    factors = [array.reshape(array.shape[2:]) for array in (factor_one, factor_two, factor_three, factor_four)]
    links = [array.reshape(array.shape[2:]) for array in (link_two, link_three, link_four)]
    sizes = tuple(factor.shape[1] for factor in factors)
    owned = tuple(factor.shape[0] for factor in factors)
    starts, height = packed_layout(factors, links)
    heights = {3: height, 2: starts["f3"], 1: starts["f2"]}
    axes = ("gx", "gy")
    core = gy_bits
    rhs_count = rhs_leaf.shape[2]

    (packed,) = vmem_call(
        functools.partial(pack_body, starts),
        [((height, LANES), jnp.float32)],
        factor_one, factor_two, factor_three, factor_four, link_two, link_three, link_four, interface,
    )
    held = [packed]
    counts = [1]
    both = [packed, from_partner(packed, axes, core)]
    strides = [(1, height), (1, height)]

    def widen(bit_number, rows):
        message = [
            block.reshape(members, -1, LANES)[:, :rows].reshape(members * rows, LANES)
            for block, members in zip(held, counts)
        ]
        message = message[0] if len(message) == 1 else jnp.concatenate(message, axis=0)
        arrived = from_partner(message, axes, bit_number)
        members = sum(counts)
        held.append(arrived)
        counts.append(members)
        both.extend([arrived, from_partner(arrived, axes, core)])
        strides.extend([(members, rows)] * 2)

    def level(section):
        rows, size = factors[section].shape
        above = sizes[section - 1] if section > 0 else 0
        members = sum(count for count, _ in strides)
        outs = [((members * rows, size), jnp.bfloat16)] * 2
        if section > 0:
            outs = outs + [((members * rows, above), jnp.bfloat16)] * 2
        body = functools.partial(gather_body, section, starts, rows, size, above, tuple(strides))
        return vmem_call(body, outs, *both)

    forward, sums = vmem_call(
        functools.partial(forward_body, sizes, owned, taken),
        [((rhs_count, rhs_leaf.shape[3]), jnp.float32), ((rhs_count, sum(sizes)), jnp.float32)],
        rhs_leaf, leaf_inv, leaf_sub, sep_rhs, interface, coupling,
    )

    inner = [bit_number for bit_number in taken[3] if bit_number != core]
    steps = {3: inner, 2: [gy_bits + gx_bits - 2], 1: [gy_bits - 1], 0: [gy_bits + gx_bits - 1]}
    sums = sums + from_partner(sums, axes, core)
    tables = [None] * 4
    found = [None] * 4
    for section in (3, 2, 1):
        for position, bit_number in enumerate(steps[section]):
            widen(bit_number, heights[section])
            theirs = from_partner(sums, axes, bit_number)
            if position < len(steps[section]) - 1:
                sums = sums + theirs
        tables[section] = level(section)
        size, above = sizes[section], sizes[section - 1]
        sums, found[section] = vmem_call(
            functools.partial(eliminate_body, size, above),
            [((rhs_count, sums.shape[1] - size), jnp.float32), ((rhs_count, size), jnp.float32)],
            sums, theirs, *tables[section],
        )
    tables[0] = level(0)
    theirs = from_partner(sums, axes, steps[0][0])
    (partial,) = vmem_call(top_body, [((rhs_count, sizes[0]), jnp.float32)], sums, theirs, *tables[0])
    theirs = from_partner(partial, axes, steps[0][0])
    leaf, sep = vmem_call(
        functools.partial(backward_body, sizes, owned, taken),
        [(rhs_leaf.shape, jnp.float32), (sep_rhs.shape, jnp.float32)],
        partial, theirs, *found[1:], *tables[1], *tables[2], *tables[3],
        forward, coupling, interface, leaf_inv, leaf_sub,
    )
    return (leaf, sep)


def local(*arrays):
    gathered_bytes = 0
    bits = lax.axis_size("gy").bit_length() + lax.axis_size("gx").bit_length() - 2
    for level, array in enumerate(arrays[6:10]):
        gathered_bytes += array.size * 4 << (bits - level)
    if gathered_bytes > GATHER_BYTES:
        return level_by_level(*arrays)
    return gathered(*arrays)


def solution(mesh):
    in_specs = (
        P("gx", "gy", None, None),
        P("gx", "gy", None, None, None),
        P("gx", "gy", None, None, None),
        P("gx", "gy", None, None),
        P("gx", "gy", None, None),
        P("gx", "gy", None, None, None),
        P("gx", "gy", None, None),
        P("gx", "gy", None, None),
        P("gx", "gy", None, None),
        P("gx", "gy", None, None),
        P("gx", "gy", None, None),
        P("gx", "gy", None, None),
        P("gx", "gy", None, None),
    )
    out_specs = (P("gx", "gy", None, None), P("gx", "gy", None, None))
    return jax.shard_map(local, mesh=mesh, in_specs=in_specs, out_specs=out_specs, check_vma=False)
```

```python
import functools

import jax
import jax.numpy as jnp
from jax import lax
from jax.experimental import pallas as pl
from jax.experimental.pallas import tpu as pltpu
from jax.sharding import PartitionSpec as P

PRECISE = lax.Precision.HIGHEST
LANES = 128
GATHER_BYTES = 8 * 2**20
VMEM_BYTES = 24 * 2**20
WHOLE_VMEM_BYTES = 60 * 2**20
BYTES_A_MICROSECOND = 3_690_000


def from_partner(value, axis, distance):
    return lax.ppermute(value, axis, [(i, i ^ 1 << distance) for i in range(lax.axis_size(axis))])


def taken_lists(gy_bits, gx_bits):
    first = list(range(gy_bits + gx_bits))
    second = [bit_number for bit_number in first if bit_number != gy_bits + gx_bits - 1]
    third = [bit_number for bit_number in second if bit_number != gy_bits - 1]
    fourth = [bit_number for bit_number in third if bit_number != gy_bits + gx_bits - 2]
    return [first, second, third, fourth]


def rank_in_group(device_index, taken):
    group_rank = jnp.zeros((), jnp.int32)
    for bit_number in sorted(taken, reverse=True):
        group_rank = group_rank * 2 + (device_index >> bit_number & 1)
    return group_rank


def group_total(values, section, taken):
    if section == 0:
        return lax.psum(values, ("gx", "gy"))
    for bit_number in sorted(taken, reverse=True):
        values = values + from_partner(values, ("gx", "gy"), bit_number)
    return values


def leaf_forward(right_side, inverse_blocks, lower_blocks):
    block_size = inverse_blocks.shape[1]
    results = []
    earlier = None
    for counter in range(inverse_blocks.shape[0]):
        current = right_side[:, counter * block_size : (counter + 1) * block_size]
        if counter > 0:
            current = current - jnp.dot(earlier, lower_blocks[counter - 1], precision=PRECISE)
        earlier = jnp.dot(current, inverse_blocks[counter], precision=PRECISE)
        results.append(earlier)
    return jnp.concatenate(results, axis=1)


def leaf_backward(leaf_work, inverse_blocks, lower_blocks):
    block_size = inverse_blocks.shape[1]
    block_count = inverse_blocks.shape[0]
    contract_last = (((1,), (1,)), ((), ()))
    results = [None] * block_count
    later = None
    for counter in reversed(range(block_count)):
        current = leaf_work[:, counter * block_size : (counter + 1) * block_size]
        if counter < block_count - 1:
            current = current - lax.dot_general(
                later, lower_blocks[counter], contract_last, precision=PRECISE
            )
        later = lax.dot_general(current, inverse_blocks[counter], contract_last, precision=PRECISE)
        results[counter] = later
    return jnp.concatenate(results, axis=1)


def level_by_level(
    rhs_leaf,
    leaf_inv,
    leaf_sub,
    sep_rhs,
    interface,
    coupling,
    factor_one,
    factor_two,
    factor_three,
    factor_four,
    link_two,
    link_three,
    link_four,
):
    contract_last = (((1,), (1,)), ((), ()))
    gy_bits = lax.axis_size("gy").bit_length() - 1
    gx_bits = lax.axis_size("gx").bit_length() - 1
    sections = taken_lists(gy_bits, gx_bits)
    device_index = lax.axis_index(("gx", "gy"))
    factors = (factor_one[0, 0], factor_two[0, 0], factor_three[0, 0], factor_four[0, 0])
    link_mats = (link_two[0, 0], link_three[0, 0], link_four[0, 0])
    places = interface[0, 0]
    couplings = coupling[0, 0]
    own_rhs = sep_rhs[0, 0]
    inverse_blocks = leaf_inv[0, 0]
    lower_blocks = leaf_sub[0, 0]
    forward = leaf_forward(rhs_leaf[0, 0], inverse_blocks, lower_blocks)
    rhs_count = forward.shape[0]
    offsets = [0]
    for section in range(3):
        offsets.append(offsets[-1] + factors[section].shape[0])
    ranks = [rank_in_group(device_index, taken) for taken in sections]
    own_z = [None] * 4
    for section in (3, 2, 1, 0):
        own_rows, sep_width = factors[section].shape
        partials_in = lax.dot_general(forward, couplings[section], contract_last, precision=PRECISE)
        if section < 3:
            partials_in = partials_in + jnp.dot(
                own_z[section + 1], link_mats[section], precision=PRECISE
            )
        contribution = jnp.zeros((rhs_count, sep_width), jnp.float32)
        own_part = own_rhs[:, offsets[section] : offsets[section] + own_rows]
        contribution = lax.dynamic_update_slice(
            contribution, own_part, (jnp.zeros((), jnp.int32), ranks[section] * own_rows)
        )
        contribution = contribution.at[:, places[section]].add(-partials_in)
        summed = group_total(contribution, section, sections[section])
        own_z[section] = lax.dot_general(summed, factors[section], contract_last, precision=PRECISE)
    full_sep = [None] * 4
    own_x = []
    for section in range(4):
        own_rows = factors[section].shape[0]
        update = own_z[section]
        if section > 0:
            picked = full_sep[section - 1][:, places[section - 1]]
            update = update - lax.dot_general(
                picked, link_mats[section - 1], contract_last, precision=PRECISE
            )
        partial_value = jnp.dot(update, factors[section], precision=PRECISE)
        full_sep[section] = group_total(partial_value, section, sections[section])
        own_x.append(
            lax.dynamic_slice_in_dim(full_sep[section], ranks[section] * own_rows, own_rows, 1)
        )
    leaf_work = forward
    for section in range(4):
        picked = full_sep[section][:, places[section]]
        leaf_work = leaf_work - jnp.dot(picked, couplings[section], precision=PRECISE)
    leaf_solution = leaf_backward(leaf_work, inverse_blocks, lower_blocks)
    sep_solution = jnp.concatenate(own_x, axis=1)
    return (leaf_solution[None, None], sep_solution[None, None])


def halves(value):
    high = value.astype(jnp.bfloat16)
    low = (value - high.astype(jnp.float32)).astype(jnp.bfloat16)
    return high, low


def few_rows(value):
    high = value.astype(jnp.bfloat16).astype(jnp.float32)
    return jnp.concatenate([high, value - high], axis=0).astype(jnp.bfloat16)


def times(left, right, transposed):
    dims = (((1,), (1 if transposed else 0,)), ((), ()))
    stacked = few_rows(left)
    total = None
    for piece in right:
        term = lax.dot_general(stacked, piece, dims, preferred_element_type=jnp.float32)
        total = term if total is None else total + term
    rows = left.shape[0]
    return total[:rows] + total[rows:]


def wide_times(left, right):
    left = jnp.concatenate(halves(left), axis=1)
    right_high, right_low = halves(right)
    right = jnp.concatenate(
        [jnp.concatenate([right_high] * 2, axis=1), jnp.concatenate([right_low] * 2, axis=1)], axis=0
    )
    total = lax.dot_general(left, right, (((1,), (1,)), ((), ())), preferred_element_type=jnp.float32)
    width = right.shape[0] // 2
    return total[:, :width] + total[:, width:]


def one_hot(positions, height):
    rows = lax.broadcasted_iota(jnp.int32, (height, positions.shape[1]), 0)
    return (rows == positions).astype(jnp.float32).astype(jnp.bfloat16)


def wide(ref, start, rows, chunks):
    pieces = [ref[start + chunk * rows : start + (chunk + 1) * rows, :] for chunk in range(chunks)]
    return pieces[0] if chunks == 1 else jnp.concatenate(pieces, axis=1)


def vmem_call(body, outs, *operands, microseconds, after=(), space=pltpu.VMEM, scratch=(), limit=VMEM_BYTES):
    out_shape = [jax.ShapeDtypeStruct(shape, dtype) for shape, dtype in outs]

    def kernel(*refs):
        body(*refs[: len(operands)], *refs[len(operands) + len(after) :])

    return pl.pallas_call(
        kernel,
        out_shape=out_shape,
        in_specs=[pl.BlockSpec(memory_space=space)] * len(operands)
        + [pl.BlockSpec(memory_space=pl.ANY)] * len(after),
        out_specs=[pl.BlockSpec(memory_space=pltpu.VMEM)] * len(outs),
        scratch_shapes=scratch,
        cost_estimate=pl.CostEstimate(
            flops=0, bytes_accessed=int(microseconds * BYTES_A_MICROSECOND), transcendentals=0
        ),
        compiler_params=pltpu.CompilerParams(vmem_limit_bytes=limit),
    )(*operands, *after)


def packed_layout(factors, link_mats):
    starts = {}
    at = 0
    for name, rows in (
        ("f0", factors[0].shape[0] * (factors[0].shape[1] // LANES)),
        ("f1", factors[1].shape[0] * (factors[1].shape[1] // LANES)),
        ("l1", link_mats[0].shape[0]),
        ("places", 8),
        ("f2", factors[2].shape[0] * (factors[2].shape[1] // LANES)),
        ("l2", link_mats[1].shape[0]),
        ("f3", factors[3].shape[0] * (factors[3].shape[1] // LANES)),
        ("l3", link_mats[2].shape[0]),
    ):
        starts[name] = at
        at += rows
    return starts, at


def pack_body(starts, f0, f1, f2, f3, l1, l2, l3, places, out, numbers, semaphores):
    moves = [(places.at[0, 0], numbers)]
    for name, ref in (("f0", f0), ("f1", f1), ("f2", f2), ("f3", f3)):
        rows, width = ref.shape[2:]
        for chunk in range(width // LANES):
            at = starts[name] + chunk * rows
            moves.append((ref.at[0, 0, :, pl.ds(chunk * LANES, LANES)], out.at[pl.ds(at, rows), :]))
    for name, ref in (("l1", l1), ("l2", l2), ("l3", l3)):
        moves.append((ref.at[0, 0], out.at[pl.ds(starts[name], ref.shape[2]), :]))
    copies = [
        pltpu.make_async_copy(source, target, semaphores.at[number])
        for number, (source, target) in enumerate(moves)
    ]
    for copy in copies:
        copy.start()
    copies[0].wait()
    positions = numbers[...].astype(jnp.float32)
    out[starts["places"] : starts["places"] + 8, :] = jnp.concatenate([positions, positions], axis=0)
    for copy in copies[1:]:
        copy.wait()


def own_targets(sizes, owned, taken):
    device_index = lax.axis_index("gx") * lax.axis_size("gy") + lax.axis_index("gy")
    columns = lax.broadcasted_iota(jnp.int32, (1, sum(owned)), 1)
    target = columns
    before = 0
    level_start = 0
    for section in range(4):
        rank = jnp.int32(0)
        for bit_number in sorted(taken[section], reverse=True):
            rank = rank * 2 + ((device_index >> bit_number) & 1)
        here = columns - before + (level_start + rank * owned[section])
        target = jnp.where(columns >= before, here, target)
        before += owned[section]
        level_start += sizes[section]
    return target


def forward_body(sizes, owned, taken, rhs, inverse, lower, sep_rhs, places, coupling, forward, sums):
    count, block = inverse.shape[2], inverse.shape[3]
    earlier = None
    for counter in range(count):
        current = rhs[0, 0, :, counter * block : (counter + 1) * block]
        if counter > 0:
            current = current - times(earlier, halves(lower[0, 0, counter - 1]), False)
        earlier = times(current, halves(inverse[0, 0, counter]), False)
        forward[:, counter * block : (counter + 1) * block] = earlier
    whole = forward[...]
    own = times(sep_rhs[0, 0], [one_hot(own_targets(sizes, owned, taken), sum(sizes))], True)
    at = 0
    for section in range(4):
        term = times(whole, halves(coupling[0, 0, section]), True)
        spread = times(term, [one_hot(places[0, 0, section : section + 1, :], sizes[section])], True)
        sums[:, at : at + sizes[section]] = own[:, at : at + sizes[section]] - spread
        at += sizes[section]


def gather_body(section, starts, rows, size, above, strides, *refs):
    outs = refs[len(strides) :]
    at = 0
    for ref, (members, stride) in zip(refs, strides):
        for member in range(members):
            base = member * stride
            factor = wide(ref, base + starts["f%d" % section], rows, size // LANES)
            outs[0][at : at + rows, :], outs[1][at : at + rows, :] = halves(factor)
            if section > 0:
                begin = base + starts["l%d" % section]
                link = ref[begin : begin + rows, :]
                row = base + starts["places"] + section - 1
                positions = ref[row : row + 1, :].astype(jnp.int32)
                linked = times(link, [one_hot(positions, above)], True)
                outs[2][at : at + rows, :], outs[3][at : at + rows, :] = halves(linked)
            at += rows


def eliminate_body(size, above, tables, mine, theirs, *refs):
    sums, found = refs[4 * tables :]
    width = mine.shape[1]
    total = mine[...] + theirs[...]
    right_side = total[:, width - size :]
    rest = total[:, width - size - above : width - size]
    at = 0
    for table in range(tables):
        f_high, f_low, m_high, m_low = refs[4 * table : 4 * table + 4]
        solved = times(right_side, [f_high[...], f_low[...]], True)
        found[:, at : at + solved.shape[1]] = solved
        rest = rest - times(solved, [m_high[...], m_low[...]], False)
        at += solved.shape[1]
    if width > size + above:
        sums[:, : width - size - above] = total[:, : width - size - above]
    sums[:, width - size - above :] = rest


def top_body(mine, theirs, f_high, f_low, partial):
    total = mine[...] + theirs[...]
    pieces = [f_high[...], f_low[...]]
    partial[...] = times(times(total, pieces, True), pieces, False)


def join_body(prefix, counts, *refs):
    copy = refs[len(counts)]
    copy[...] = refs[len(counts) - 1][...]
    if prefix == 0:
        return
    message = refs[len(counts) + 1]
    at = 0
    for ref, members in zip(refs, counts):
        stride = ref.shape[0] // members
        for member in range(members):
            message[at : at + prefix, :] = ref[member * stride : member * stride + prefix, :]
            at += prefix


def add_body(mine, theirs, out):
    out[...] = mine[...] + theirs[...]


def fold_body(tables, found, *refs):
    solved, n_high, n_low = refs[4 * tables :]
    dims = (((0,), (0,)), ((), ()))
    known = folded = None
    at = 0
    for table in range(tables):
        f_high, f_low, m_high, m_low = refs[4 * table : 4 * table + 4]
        rows = f_high.shape[0]
        pieces = [f_high[...], f_low[...]]
        term = times(found[:, at : at + rows], pieces, False)
        known = term if known is None else known + term
        for link in (m_high[...], m_low[...]):
            for piece in pieces:
                term = lax.dot_general(link, piece, dims, preferred_element_type=jnp.float32)
                folded = term if folded is None else folded + term
        at += rows
    solved[...] = known
    n_high[...], n_low[...] = halves(folded)


def leaf_body(sections, forward, coupling, inverse, lower, base, d_high, d_low):
    count, block = inverse.shape[2], inverse.shape[3]
    rhs_count = forward.shape[0]
    rows = [coupling[0, 0, section] for section in sections]
    rows = jnp.concatenate([forward[...]] + rows, axis=0)
    later = None
    for counter in reversed(range(count)):
        current = rows[:, counter * block : (counter + 1) * block]
        if counter < count - 1:
            current = current - wide_times(later, lower[0, 0, counter])
        later = wide_times(current, inverse[0, 0, counter])
        columns = slice(counter * block, (counter + 1) * block)
        base[:, columns] = later[:rhs_count]
        d_high[:, columns], d_low[:, columns] = halves(later[rhs_count:])


def backward_body(
    sizes, owned, taken, mine, theirs, u1, n1h, n1l, u2, n2h, n2l, u3, n3h, n3l,
    base, d1h, d1l, d2h, d2l, places, leaf, sep,
):
    solved = [mine[...] + theirs[...]]
    for known, n_high, n_low in ((u1, n1h, n1l), (u2, n2h, n2l), (u3, n3h, n3l)):
        solved.append(known[...] - times(solved[-1], [n_high[...], n_low[...]], False))
    picked = [
        times(solved[section], [one_hot(places[0, 0, section : section + 1, :], sizes[section])], False)
        for section in range(4)
    ]
    first = times(jnp.concatenate(picked[:2], axis=1), [d1h[...], d1l[...]], False)
    second = times(jnp.concatenate(picked[2:], axis=1), [d2h[...], d2l[...]], False)
    leaf[0, 0] = base[...] - first - second
    everything = jnp.concatenate(solved, axis=1)
    sep[0, 0] = times(everything, [one_hot(own_targets(sizes, owned, taken), sum(sizes))], False)


def gathered(
    rhs_leaf,
    leaf_inv,
    leaf_sub,
    sep_rhs,
    interface,
    coupling,
    factor_one,
    factor_two,
    factor_three,
    factor_four,
    link_two,
    link_three,
    link_four,
):
    gy_bits = lax.axis_size("gy").bit_length() - 1
    gx_bits = lax.axis_size("gx").bit_length() - 1
    taken = taken_lists(gy_bits, gx_bits)
    factors = [array.reshape(array.shape[2:]) for array in (factor_one, factor_two, factor_three, factor_four)]
    links = [array.reshape(array.shape[2:]) for array in (link_two, link_three, link_four)]
    sizes = tuple(factor.shape[1] for factor in factors)
    owned = tuple(factor.shape[0] for factor in factors)
    starts, height = packed_layout(factors, links)
    heights = {3: height, 2: starts["f3"], 1: starts["f2"]}
    axes = ("gx", "gy")
    core = gy_bits
    rhs_count = rhs_leaf.shape[2]
    copies = 1 + sum(size // LANES for size in sizes) + len(links)

    (packed,) = vmem_call(
        functools.partial(pack_body, starts),
        [((height, LANES), jnp.float32)],
        factor_one, factor_two, factor_three, factor_four, link_two, link_three, link_four, interface,
        microseconds=1.0, space=pltpu.HBM, limit=WHOLE_VMEM_BYTES,
        scratch=(pltpu.VMEM(interface.shape[2:], jnp.int32), pltpu.SemaphoreType.DMA((copies,))),
    )
    held = [packed]
    counts = [1]
    both = [packed, from_partner(packed, axes, core)]
    strides = [(1, height), (1, height)]

    def arrive(arrived, stride, prefix, after):
        held.append(arrived)
        counts.append(arrived.shape[0] // stride)
        outs = [(arrived.shape, jnp.float32)]
        if prefix:
            outs.append(((sum(counts) * prefix, LANES), jnp.float32))
        copy, *message = vmem_call(
            functools.partial(join_body, prefix, tuple(counts)), outs, *held, after=after, microseconds=0.1
        )
        held[-1] = copy
        both.extend([copy, from_partner(copy, axes, core)])
        strides.extend([(counts[-1], stride)] * 2)
        return message

    def level(section, first, last, after=()):
        rows, size = factors[section].shape
        above = sizes[section - 1] if section > 0 else 0
        members = sum(count for count, _ in strides[first:last])
        outs = [((members * rows, size), jnp.bfloat16)] * 2
        if section > 0:
            outs = outs + [((members * rows, above), jnp.bfloat16)] * 2
        body = functools.partial(gather_body, section, starts, rows, size, above, tuple(strides[first:last]))
        return vmem_call(body, outs, *both[first:last], microseconds=0.4, after=after)

    inner = [bit_number for bit_number in taken[3] if bit_number != core]
    steps = [(bit_number, 3) for bit_number in inner]
    steps += [(gy_bits + gx_bits - 2, 2), (gy_bits - 1, 1)]
    moving = from_partner(packed, axes, steps[0][0])
    forward, sums = vmem_call(
        functools.partial(forward_body, sizes, owned, taken),
        [((rhs_count, rhs_leaf.shape[3]), jnp.float32), ((rhs_count, sum(sizes)), jnp.float32)],
        rhs_leaf, leaf_inv, leaf_sub, sep_rhs, interface, coupling, microseconds=2.0,
    )
    (sums,) = vmem_call(
        add_body, [((rhs_count, sum(sizes)), jnp.float32)], sums, from_partner(sums, axes, core), microseconds=0.1
    )
    folded = [None] * 4
    late = ()
    for number, (bit_number, section) in enumerate(steps):
        theirs = from_partner(sums, axes, bit_number)
        following = steps[number + 1] if number + 1 < len(steps) else (None, None)
        prefix = heights[following[1]] if following[1] else 0
        known = len(both)
        message = arrive(moving, heights[section], prefix, (sums,))
        if message:
            moving = from_partner(message[0], axes, following[0])
        if following[1] == section:
            sums = sums + theirs
            continue
        if section == 1:
            tables = [level(section, 0, known, (sums,)), level(section, known, len(both))]
        else:
            tables = [level(section, 0, len(both))]
        size, above = sizes[section], sizes[section - 1]
        flat = [array for table in tables for array in table]
        sums, found = vmem_call(
            functools.partial(eliminate_body, size, above, len(tables)),
            [((rhs_count, sums.shape[1] - size), jnp.float32), ((rhs_count, size), jnp.float32)],
            sums, theirs, *flat, microseconds=0.4, after=late,
        )
        folded[section] = vmem_call(
            functools.partial(fold_body, len(tables)),
            [((rhs_count, size), jnp.float32)] + [((above, size), jnp.bfloat16)] * 2,
            found, *flat, microseconds=0.5,
        )
        late = tuple(folded[section][:1])
    last = gy_bits + gx_bits - 1
    solves = [
        vmem_call(
            functools.partial(leaf_body, sections),
            [((rhs_count, rhs_leaf.shape[3]), jnp.float32)] + [((2 * LANES, rhs_leaf.shape[3]), jnp.bfloat16)] * 2,
            forward, coupling, leaf_inv, leaf_sub, microseconds=1.0, after=(before,),
        )
        for sections, before in (((0, 1), sums), ((2, 3), sums))
    ]
    table = level(0, 0, len(both))
    theirs = from_partner(sums, axes, last)
    (partial,) = vmem_call(
        top_body, [((rhs_count, sizes[0]), jnp.float32)],
        sums, theirs, *table, microseconds=0.5, after=(solves[0][0],),
    )
    theirs = from_partner(partial, axes, last)
    leaf, sep = vmem_call(
        functools.partial(backward_body, sizes, owned, taken),
        [(rhs_leaf.shape, jnp.float32), (sep_rhs.shape, jnp.float32)],
        partial, theirs, *folded[1], *folded[2], *folded[3], *solves[0], *solves[1][1:], interface,
        microseconds=2.0,
    )
    return (leaf, sep)


def local(*arrays):
    gathered_bytes = 0
    bits = lax.axis_size("gy").bit_length() + lax.axis_size("gx").bit_length() - 2
    for level, array in enumerate(arrays[6:10]):
        gathered_bytes += array.size * 4 << (bits - level)
    if gathered_bytes > GATHER_BYTES:
        return level_by_level(*arrays)
    return gathered(*arrays)


def solution(mesh):
    in_specs = (
        P("gx", "gy", None, None),
        P("gx", "gy", None, None, None),
        P("gx", "gy", None, None, None),
        P("gx", "gy", None, None),
        P("gx", "gy", None, None),
        P("gx", "gy", None, None, None),
        P("gx", "gy", None, None),
        P("gx", "gy", None, None),
        P("gx", "gy", None, None),
        P("gx", "gy", None, None),
        P("gx", "gy", None, None),
        P("gx", "gy", None, None),
        P("gx", "gy", None, None),
    )
    out_specs = (P("gx", "gy", None, None), P("gx", "gy", None, None))
    return jax.shard_map(local, mesh=mesh, in_specs=in_specs, out_specs=out_specs, check_vma=False)
```

```python
import functools

import jax
import jax.numpy as jnp
from jax import lax
from jax.experimental import pallas as pl
from jax.experimental.pallas import tpu as pltpu
from jax.sharding import PartitionSpec as P

PRECISE = lax.Precision.HIGHEST
LANES = 128
GATHER_BYTES = 8 * 2**20
VMEM_BYTES = 24 * 2**20
WHOLE_VMEM_BYTES = 60 * 2**20
FLOPS_A_MICROSECOND = 1_000_000_000
ARRIVE_US = 0.1
SOLVE_US = 2.0
X2_US = 5.0
NEAR_US = 5.0
Y2_US = 5.0
LAST_US = 0.1
F1_US = 5.0
F1C_US = 0.1
SUM_US = 5.0
TABLE_US = 0.4
FOLD_US = 0.5
LEAF_US = 1.0
ELIM_US = 5.0


def from_partner(value, axis, distance):
    return lax.ppermute(value, axis, [(i, i ^ 1 << distance) for i in range(lax.axis_size(axis))])


def taken_lists(gy_bits, gx_bits):
    first = list(range(gy_bits + gx_bits))
    second = [bit_number for bit_number in first if bit_number != gy_bits + gx_bits - 1]
    third = [bit_number for bit_number in second if bit_number != gy_bits - 1]
    fourth = [bit_number for bit_number in third if bit_number != gy_bits + gx_bits - 2]
    return [first, second, third, fourth]


def rank_in_group(device_index, taken):
    group_rank = jnp.zeros((), jnp.int32)
    for bit_number in sorted(taken, reverse=True):
        group_rank = group_rank * 2 + (device_index >> bit_number & 1)
    return group_rank


def group_total(values, section, taken):
    if section == 0:
        return lax.psum(values, ("gx", "gy"))
    for bit_number in sorted(taken, reverse=True):
        values = values + from_partner(values, ("gx", "gy"), bit_number)
    return values


def leaf_forward(right_side, inverse_blocks, lower_blocks):
    block_size = inverse_blocks.shape[1]
    results = []
    earlier = None
    for counter in range(inverse_blocks.shape[0]):
        current = right_side[:, counter * block_size : (counter + 1) * block_size]
        if counter > 0:
            current = current - jnp.dot(earlier, lower_blocks[counter - 1], precision=PRECISE)
        earlier = jnp.dot(current, inverse_blocks[counter], precision=PRECISE)
        results.append(earlier)
    return jnp.concatenate(results, axis=1)


def leaf_backward(leaf_work, inverse_blocks, lower_blocks):
    block_size = inverse_blocks.shape[1]
    block_count = inverse_blocks.shape[0]
    contract_last = (((1,), (1,)), ((), ()))
    results = [None] * block_count
    later = None
    for counter in reversed(range(block_count)):
        current = leaf_work[:, counter * block_size : (counter + 1) * block_size]
        if counter < block_count - 1:
            current = current - lax.dot_general(
                later, lower_blocks[counter], contract_last, precision=PRECISE
            )
        later = lax.dot_general(current, inverse_blocks[counter], contract_last, precision=PRECISE)
        results[counter] = later
    return jnp.concatenate(results, axis=1)


def level_by_level(
    rhs_leaf,
    leaf_inv,
    leaf_sub,
    sep_rhs,
    interface,
    coupling,
    factor_one,
    factor_two,
    factor_three,
    factor_four,
    link_two,
    link_three,
    link_four,
):
    contract_last = (((1,), (1,)), ((), ()))
    gy_bits = lax.axis_size("gy").bit_length() - 1
    gx_bits = lax.axis_size("gx").bit_length() - 1
    sections = taken_lists(gy_bits, gx_bits)
    device_index = lax.axis_index(("gx", "gy"))
    factors = (factor_one[0, 0], factor_two[0, 0], factor_three[0, 0], factor_four[0, 0])
    link_mats = (link_two[0, 0], link_three[0, 0], link_four[0, 0])
    places = interface[0, 0]
    couplings = coupling[0, 0]
    own_rhs = sep_rhs[0, 0]
    inverse_blocks = leaf_inv[0, 0]
    lower_blocks = leaf_sub[0, 0]
    forward = leaf_forward(rhs_leaf[0, 0], inverse_blocks, lower_blocks)
    rhs_count = forward.shape[0]
    offsets = [0]
    for section in range(3):
        offsets.append(offsets[-1] + factors[section].shape[0])
    ranks = [rank_in_group(device_index, taken) for taken in sections]
    own_z = [None] * 4
    for section in (3, 2, 1, 0):
        own_rows, sep_width = factors[section].shape
        partials_in = lax.dot_general(forward, couplings[section], contract_last, precision=PRECISE)
        if section < 3:
            partials_in = partials_in + jnp.dot(
                own_z[section + 1], link_mats[section], precision=PRECISE
            )
        contribution = jnp.zeros((rhs_count, sep_width), jnp.float32)
        own_part = own_rhs[:, offsets[section] : offsets[section] + own_rows]
        contribution = lax.dynamic_update_slice(
            contribution, own_part, (jnp.zeros((), jnp.int32), ranks[section] * own_rows)
        )
        contribution = contribution.at[:, places[section]].add(-partials_in)
        summed = group_total(contribution, section, sections[section])
        own_z[section] = lax.dot_general(summed, factors[section], contract_last, precision=PRECISE)
    full_sep = [None] * 4
    own_x = []
    for section in range(4):
        own_rows = factors[section].shape[0]
        update = own_z[section]
        if section > 0:
            picked = full_sep[section - 1][:, places[section - 1]]
            update = update - lax.dot_general(
                picked, link_mats[section - 1], contract_last, precision=PRECISE
            )
        partial_value = jnp.dot(update, factors[section], precision=PRECISE)
        full_sep[section] = group_total(partial_value, section, sections[section])
        own_x.append(
            lax.dynamic_slice_in_dim(full_sep[section], ranks[section] * own_rows, own_rows, 1)
        )
    leaf_work = forward
    for section in range(4):
        picked = full_sep[section][:, places[section]]
        leaf_work = leaf_work - jnp.dot(picked, couplings[section], precision=PRECISE)
    leaf_solution = leaf_backward(leaf_work, inverse_blocks, lower_blocks)
    sep_solution = jnp.concatenate(own_x, axis=1)
    return (leaf_solution[None, None], sep_solution[None, None])


def halves(value):
    high = value.astype(jnp.bfloat16)
    low = (value - high.astype(jnp.float32)).astype(jnp.bfloat16)
    return high, low


def few_rows(value):
    high = value.astype(jnp.bfloat16).astype(jnp.float32)
    return jnp.concatenate([high, value - high], axis=0).astype(jnp.bfloat16)


def times(left, right, transposed):
    dims = (((1,), (1 if transposed else 0,)), ((), ()))
    stacked = few_rows(left)
    total = None
    for piece in right:
        term = lax.dot_general(stacked, piece, dims, preferred_element_type=jnp.float32)
        total = term if total is None else total + term
    rows = left.shape[0]
    return total[:rows] + total[rows:]


def wide_times(left, right):
    left = jnp.concatenate(halves(left), axis=1)
    right_high, right_low = halves(right)
    right = jnp.concatenate(
        [jnp.concatenate([right_high] * 2, axis=1), jnp.concatenate([right_low] * 2, axis=1)], axis=0
    )
    total = lax.dot_general(left, right, (((1,), (1,)), ((), ())), preferred_element_type=jnp.float32)
    width = right.shape[0] // 2
    return total[:, :width] + total[:, width:]


def one_hot(positions, height):
    rows = lax.broadcasted_iota(jnp.int32, (height, positions.shape[1]), 0)
    return (rows == positions).astype(jnp.float32).astype(jnp.bfloat16)


def wide(ref, start, rows, chunks):
    pieces = [ref[start + chunk * rows : start + (chunk + 1) * rows, :] for chunk in range(chunks)]
    return pieces[0] if chunks == 1 else jnp.concatenate(pieces, axis=1)


def vmem_call(body, outs, *operands, microseconds, after=(), space=pltpu.VMEM, scratch=(), limit=VMEM_BYTES):
    out_shape = [jax.ShapeDtypeStruct(shape, dtype) for shape, dtype in outs]

    def kernel(*refs):
        body(*refs[: len(operands)], *refs[len(operands) + len(after) :])

    return pl.pallas_call(
        kernel,
        out_shape=out_shape,
        in_specs=[pl.BlockSpec(memory_space=space)] * len(operands)
        + [pl.BlockSpec(memory_space=pl.ANY)] * len(after),
        out_specs=[pl.BlockSpec(memory_space=pltpu.VMEM)] * len(outs),
        scratch_shapes=scratch,
        cost_estimate=pl.CostEstimate(
            flops=int(microseconds * FLOPS_A_MICROSECOND), bytes_accessed=0, transcendentals=0
        ),
        compiler_params=pltpu.CompilerParams(vmem_limit_bytes=limit),
    )(*operands, *after)


def packed_layout(factors, link_mats):
    starts = {}
    sets = []
    at = 0
    for section, names in enumerate((("f0",), ("f1", "l1", "places"), ("f2", "l2"), ("f3", "l3"))):
        begin = at
        for name in names:
            starts[name] = at
            if name == "places":
                at += 8
            elif name[0] == "f":
                at += factors[section].shape[0] * (factors[section].shape[1] // LANES)
            else:
                at += link_mats[section - 1].shape[0]
        sets.append((begin, at))
    return starts, tuple(sets), at


def pack_body(starts, part, f0, f1, f2, f3, l1, l2, l3, places, out, tail, s0, s1, s2, numbers, semaphores):
    moves = [(places.at[0, 0], numbers), (f0.at[0, 0], s0), (f1.at[0, 0], s1), (f2.at[0, 0], s2)]
    for name, ref in (("f3", f3), ("l1", l1), ("l2", l2), ("l3", l3)):
        moves.append((ref.at[0, 0], out.at[pl.ds(starts[name], ref.shape[2]), :]))
    copies = [
        pltpu.make_async_copy(source, target, semaphores.at[number])
        for number, (source, target) in enumerate(moves)
    ]
    for copy in copies:
        copy.start()
    for copy in copies[:4]:
        copy.wait()
    positions = numbers[...].astype(jnp.float32)
    out[starts["places"] : starts["places"] + 8, :] = jnp.concatenate([positions, positions], axis=0)
    for name, ref in (("f0", s0), ("f1", s1), ("f2", s2)):
        rows, width = ref.shape
        for chunk in range(width // LANES):
            at = starts[name] + chunk * rows
            out[at : at + rows, :] = ref[:, chunk * LANES : (chunk + 1) * LANES]
    for copy in copies[4:]:
        copy.wait()
    tail[...] = out[part[0] : part[1], :]


def own_targets(sizes, owned, taken):
    device_index = lax.axis_index("gx") * lax.axis_size("gy") + lax.axis_index("gy")
    columns = lax.broadcasted_iota(jnp.int32, (1, sum(owned)), 1)
    target = columns
    before = 0
    level_start = 0
    for section in range(4):
        rank = jnp.int32(0)
        for bit_number in sorted(taken[section], reverse=True):
            rank = rank * 2 + ((device_index >> bit_number) & 1)
        here = columns - before + (level_start + rank * owned[section])
        target = jnp.where(columns >= before, here, target)
        before += owned[section]
        level_start += sizes[section]
    return target


def forward_body(sizes, owned, taken, rhs, inverse, lower, sep_rhs, places, coupling, forward, sums):
    count, block = inverse.shape[2], inverse.shape[3]
    earlier = None
    for counter in range(count):
        current = rhs[0, 0, :, counter * block : (counter + 1) * block]
        if counter > 0:
            current = current - times(earlier, halves(lower[0, 0, counter - 1]), False)
        earlier = times(current, halves(inverse[0, 0, counter]), False)
        forward[:, counter * block : (counter + 1) * block] = earlier
    whole = forward[...]
    own = times(sep_rhs[0, 0], [one_hot(own_targets(sizes, owned, taken), sum(sizes))], True)
    at = 0
    for section in range(4):
        term = times(whole, halves(coupling[0, 0, section]), True)
        spread = times(term, [one_hot(places[0, 0, section : section + 1, :], sizes[section])], True)
        sums[:, at : at + sizes[section]] = own[:, at : at + sizes[section]] - spread
        at += sizes[section]


def gather_body(section, starts, rows, size, above, places, *refs):
    outs = refs[len(places) :]
    at = 0
    for ref, bases in zip(refs, places):
        for base in bases:
            factor = wide(ref, base + starts["f%d" % section], rows, size // LANES)
            outs[0][at : at + rows, :], outs[1][at : at + rows, :] = halves(factor)
            if section > 0:
                place = base + starts["l%d" % section]
                link = ref[place : place + rows, :]
                row = base + starts["places"] + section - 1
                positions = ref[row : row + 1, :].astype(jnp.int32)
                linked = times(link, [one_hot(positions, above)], True)
                outs[2][at : at + rows, :], outs[3][at : at + rows, :] = halves(linked)
            at += rows


def eliminate_body(size, above, tables, mine, theirs, *refs):
    sums, found = refs[4 * tables :]
    width = mine.shape[1]
    total = mine[...] + theirs[...]
    right_side = total[:, width - size :]
    rest = total[:, width - size - above : width - size]
    at = 0
    for table in range(tables):
        f_high, f_low, m_high, m_low = refs[4 * table : 4 * table + 4]
        solved = times(right_side, [f_high[...], f_low[...]], True)
        found[:, at : at + solved.shape[1]] = solved
        rest = rest - times(solved, [m_high[...], m_low[...]], False)
        at += solved.shape[1]
    if width > size + above:
        sums[:, : width - size - above] = total[:, : width - size - above]
    sums[:, width - size - above :] = rest


def top_body(total, f_high, f_low, partial):
    pieces = [f_high[...], f_low[...]]
    partial[...] = times(times(total[...], pieces, True), pieces, False)


def join_body(moves, *refs):
    for number, start, at, rows in moves:
        refs[-1][at : at + rows, :] = refs[number][start : start + rows, :]


def copy_body(arrived, out):
    out[...] = arrived[...]


def add_body(mine, theirs, out):
    out[...] = mine[...] + theirs[...]


def fold_body(tables, found, *refs):
    solved, n_high, n_low = refs[4 * tables :]
    dims = (((0,), (0,)), ((), ()))
    known = folded = None
    at = 0
    for table in range(tables):
        f_high, f_low, m_high, m_low = refs[4 * table : 4 * table + 4]
        rows = f_high.shape[0]
        pieces = [f_high[...], f_low[...]]
        term = times(found[:, at : at + rows], pieces, False)
        known = term if known is None else known + term
        for link in (m_high[...], m_low[...]):
            for piece in pieces:
                term = lax.dot_general(link, piece, dims, preferred_element_type=jnp.float32)
                folded = term if folded is None else folded + term
        at += rows
    solved[...] = known
    n_high[...], n_low[...] = halves(folded)


def leaf_body(sections, forward, coupling, inverse, lower, base, d_high, d_low):
    count, block = inverse.shape[2], inverse.shape[3]
    rhs_count = forward.shape[0]
    rows = [coupling[0, 0, section] for section in sections]
    rows = jnp.concatenate([forward[...]] + rows, axis=0)
    later = None
    for counter in reversed(range(count)):
        current = rows[:, counter * block : (counter + 1) * block]
        if counter < count - 1:
            current = current - wide_times(later, lower[0, 0, counter])
        later = wide_times(current, inverse[0, 0, counter])
        columns = slice(counter * block, (counter + 1) * block)
        base[:, columns] = later[:rhs_count]
        d_high[:, columns], d_low[:, columns] = halves(later[rhs_count:])


def backward_body(
    sizes, owned, taken, mine, theirs, u1, n1h, n1l, u2, n2h, n2l, u3, n3h, n3l,
    base, d1h, d1l, d2h, d2l, places, leaf, sep,
):
    solved = [mine[...] + theirs[...]]
    for known, n_high, n_low in ((u1, n1h, n1l), (u2, n2h, n2l), (u3, n3h, n3l)):
        solved.append(known[...] - times(solved[-1], [n_high[...], n_low[...]], False))
    picked = [
        times(solved[section], [one_hot(places[0, 0, section : section + 1, :], sizes[section])], False)
        for section in range(4)
    ]
    first = times(jnp.concatenate(picked[:2], axis=1), [d1h[...], d1l[...]], False)
    second = times(jnp.concatenate(picked[2:], axis=1), [d2h[...], d2l[...]], False)
    leaf[0, 0] = base[...] - first - second
    everything = jnp.concatenate(solved, axis=1)
    sep[0, 0] = times(everything, [one_hot(own_targets(sizes, owned, taken), sum(sizes))], False)


def gathered(
    rhs_leaf,
    leaf_inv,
    leaf_sub,
    sep_rhs,
    interface,
    coupling,
    factor_one,
    factor_two,
    factor_three,
    factor_four,
    link_two,
    link_three,
    link_four,
):
    gy_bits = lax.axis_size("gy").bit_length() - 1
    gx_bits = lax.axis_size("gx").bit_length() - 1
    taken = taken_lists(gy_bits, gx_bits)
    factors = [array.reshape(array.shape[2:]) for array in (factor_one, factor_two, factor_three, factor_four)]
    links = [array.reshape(array.shape[2:]) for array in (link_two, link_three, link_four)]
    sizes = tuple(factor.shape[1] for factor in factors)
    owned = tuple(factor.shape[0] for factor in factors)
    starts, sets, height = packed_layout(factors, links)
    axes = ("gx", "gy")
    core = gy_bits
    rhs_count = rhs_leaf.shape[2]
    total = sum(sizes)

    part = (sets[1][0], sets[2][1])
    packed, tail = vmem_call(
        functools.partial(pack_body, starts, part),
        [((height, LANES), jnp.float32), ((part[1] - part[0], LANES), jnp.float32)],
        factor_one, factor_two, factor_three, factor_four, link_two, link_three, link_four, interface,
        microseconds=1.0, space=pltpu.HBM, limit=WHOLE_VMEM_BYTES,
        scratch=[pltpu.VMEM(factor.shape, jnp.float32) for factor in factors[:3]]
        + [pltpu.VMEM(interface.shape[2:], jnp.int32), pltpu.SemaphoreType.DMA((8,))],
    )

    everything = (0, 1, 2, 3)
    whole = ((0, everything),)
    both = [(packed, whole), (from_partner(packed, axes, core), whole)]

    def plan(wanted):
        moves, members, at = [], [], 0
        for number, (_, have) in enumerate(wanted):
            for base, its_sets, travels in have:
                first, last = sets[travels[0]][0], sets[travels[-1]][1]
                moves.append((number, base + first, at, last - first))
                members.append((at - first, travels))
                at += last - first
        return tuple(moves), tuple(members), at

    def choose(buffers, *travels):
        wanted = []
        for array, members in buffers:
            have = []
            for base, its_sets in members:
                fit = [run for run in travels if set(run) <= set(its_sets)]
                if fit:
                    have.append((base, its_sets, fit[0]))
            if have:
                wanted.append((array, tuple(have)))
        return wanted

    def message(wanted, after, microseconds=ARRIVE_US):
        moves, members, rows = plan(wanted)
        (out,) = vmem_call(
            functools.partial(join_body, moves), [((rows, LANES), jnp.float32)],
            *[array for array, _ in wanted], after=after, microseconds=microseconds,
        )
        return out, members

    def arrive(arrived, members, after, microseconds=ARRIVE_US):
        (copy,) = vmem_call(
            copy_body, [(arrived.shape, jnp.float32)], arrived, after=after, microseconds=microseconds
        )
        both.extend([(copy, members), (from_partner(copy, axes, core), members)])
        return copy, members

    def level(section, buffers, after=()):
        rows, size = factors[section].shape
        above = sizes[section - 1] if section > 0 else 0
        chosen = choose(buffers, (section,))
        places = tuple(tuple(base for base, _, _ in have) for _, have in chosen)
        count = sum(len(bases) for bases in places)
        outs = [((count * rows, size), jnp.bfloat16)] * 2
        if section > 0:
            outs = outs + [((count * rows, above), jnp.bfloat16)] * 2
        body = functools.partial(gather_body, section, starts, rows, size, above, places)
        return vmem_call(body, outs, *[array for array, _ in chosen], microseconds=TABLE_US, after=after)

    def eliminate(section, sums, theirs, tables, after):
        size, above = sizes[section], sizes[section - 1]
        flat = [array for table in tables for array in table]
        sums, found = vmem_call(
            functools.partial(eliminate_body, size, above, len(tables)),
            [((rhs_count, sums.shape[1] - size), jnp.float32), ((rhs_count, size), jnp.float32)],
            sums, theirs, *flat, microseconds=ELIM_US, after=after,
        )
        folded = vmem_call(
            functools.partial(fold_body, len(tables)),
            [((rhs_count, size), jnp.float32)] + [((above, size), jnp.bfloat16)] * 2,
            found, *flat, microseconds=FOLD_US,
        )
        return sums, folded

    def solve(sections, after):
        return vmem_call(
            functools.partial(leaf_body, sections),
            [((rhs_count, rhs_leaf.shape[3]), jnp.float32)]
            + [((len(sections) * LANES, rhs_leaf.shape[3]), jnp.bfloat16)] * 2,
            forward, coupling, leaf_inv, leaf_sub, microseconds=LEAF_US, after=after,
        )

    inner = min(taken[3]) if core == max(taken[3]) else max(taken[3])
    third, second, first = gy_bits + gx_bits - 2, gy_bits - 1, gy_bits + gx_bits - 1

    from_inner = from_partner(packed, axes, inner)
    from_third = from_partner(tail, axes, third)
    forward, sums = vmem_call(
        functools.partial(forward_body, sizes, owned, taken),
        [((rhs_count, rhs_leaf.shape[3]), jnp.float32), ((rhs_count, total), jnp.float32)],
        rhs_leaf, leaf_inv, leaf_sub, sep_rhs, interface, coupling, microseconds=SOLVE_US,
    )
    others = from_partner(sums, axes, core)
    by_third = arrive(from_third, ((-part[0], (1, 2)),), ())
    (sums,) = vmem_call(
        add_body, [((rhs_count, total), jnp.float32)], sums, others, microseconds=0.1, after=(by_third[0],)
    )
    theirs = from_partner(sums, axes, inner)
    by_inner = arrive(from_inner, whole, (sums,))
    following, two_at = message(choose([by_third], (1, 2)), (sums,))
    two = from_partner(following, axes, inner)
    following, near_at = message(choose([both[0], by_inner], (0, 1)), (sums,))
    near = from_partner(following, axes, second)
    table = level(3, both)
    sums, folded_four = eliminate(3, sums, theirs, [table], ())

    theirs = from_partner(sums, axes, third)
    solved_first = solve((0, 1), (sums,))
    by_two = arrive(two, two_at, (solved_first[0],), X2_US)
    by_near = arrive(near, near_at, (solved_first[0],), NEAR_US)
    following, last_at = message(choose([by_third, by_two], (1,)), (sums,), Y2_US)
    last = from_partner(following, axes, second)
    table = level(2, both)
    sums, folded_three = eliminate(2, sums, theirs, [table], (folded_four[0],))

    theirs = from_partner(sums, axes, second)
    following, top_at = message(choose([both[0], by_inner, by_near], (0,)), (sums,), F1_US)
    from_third = from_partner(following, axes, third)
    early = len(both)
    arrive(last, last_at, (sums,), LAST_US)
    tables = [level(1, both[:early], (sums,)), level(1, both[early:], (sums,))]
    sums, folded_two = eliminate(1, sums, theirs, tables, (folded_three[0],))

    theirs = from_partner(sums, axes, first)
    arrive(from_third, top_at, (sums,), F1C_US)
    (sums,) = vmem_call(
        add_body, [((rhs_count, sizes[0]), jnp.float32)], sums, theirs, microseconds=SUM_US
    )
    (partial,) = vmem_call(
        top_body, [((rhs_count, sizes[0]), jnp.float32)], sums, *level(0, both, (sums,)), microseconds=0.5
    )
    theirs = from_partner(partial, axes, first)
    solved_second = solve((2, 3), (partial,))
    leaf, sep = vmem_call(
        functools.partial(backward_body, sizes, owned, taken),
        [(rhs_leaf.shape, jnp.float32), (sep_rhs.shape, jnp.float32)],
        partial, theirs, *folded_two, *folded_three, *folded_four, *solved_first, *solved_second[1:], interface,
        microseconds=2.0,
    )
    return (leaf, sep)


def local(*arrays):
    gathered_bytes = 0
    bits = lax.axis_size("gy").bit_length() + lax.axis_size("gx").bit_length() - 2
    for level, array in enumerate(arrays[6:10]):
        gathered_bytes += array.size * 4 << (bits - level)
    gy_bits = lax.axis_size("gy").bit_length() - 1
    fourth = taken_lists(gy_bits, bits - gy_bits)[3]
    if gathered_bytes > GATHER_BYTES or len(fourth) != 2 or gy_bits not in fourth:
        return level_by_level(*arrays)
    return gathered(*arrays)


def solution(mesh):
    in_specs = (
        P("gx", "gy", None, None),
        P("gx", "gy", None, None, None),
        P("gx", "gy", None, None, None),
        P("gx", "gy", None, None),
        P("gx", "gy", None, None),
        P("gx", "gy", None, None, None),
        P("gx", "gy", None, None),
        P("gx", "gy", None, None),
        P("gx", "gy", None, None),
        P("gx", "gy", None, None),
        P("gx", "gy", None, None),
        P("gx", "gy", None, None),
        P("gx", "gy", None, None),
    )
    out_specs = (P("gx", "gy", None, None), P("gx", "gy", None, None))
    return jax.shard_map(local, mesh=mesh, in_specs=in_specs, out_specs=out_specs, check_vma=False)
```

```python
import functools

import jax
import jax.numpy as jnp
from jax import lax
from jax.experimental import pallas as pl
from jax.experimental.pallas import tpu as pltpu
from jax.sharding import PartitionSpec as P

PRECISE = lax.Precision.HIGHEST
LANES = 128
GATHER_BYTES = 8 * 2**20
VMEM_BYTES = 24 * 2**20
FLOPS_A_MICROSECOND = 1_000_000_000
ARRIVE_US = 0.1
SOLVE_US = 2.0
X2_US = 5.0
NEAR_US = 5.0
Y2_US = 5.0
LAST_US = 0.1
F1_US = 5.0
F1C_US = 0.1
SUM_US = 5.0
TABLE_US = 0.4
FOLD_US = 0.5
LEAF_US = 1.0
ELIM_US = 5.0


def from_partner(value, axis, distance):
    return lax.ppermute(value, axis, [(i, i ^ 1 << distance) for i in range(lax.axis_size(axis))])


def taken_lists(gy_bits, gx_bits):
    first = list(range(gy_bits + gx_bits))
    second = [bit_number for bit_number in first if bit_number != gy_bits + gx_bits - 1]
    third = [bit_number for bit_number in second if bit_number != gy_bits - 1]
    fourth = [bit_number for bit_number in third if bit_number != gy_bits + gx_bits - 2]
    return [first, second, third, fourth]


def rank_in_group(device_index, taken):
    group_rank = jnp.zeros((), jnp.int32)
    for bit_number in sorted(taken, reverse=True):
        group_rank = group_rank * 2 + (device_index >> bit_number & 1)
    return group_rank


def group_total(values, section, taken):
    if section == 0:
        return lax.psum(values, ("gx", "gy"))
    for bit_number in sorted(taken, reverse=True):
        values = values + from_partner(values, ("gx", "gy"), bit_number)
    return values


def leaf_forward(right_side, inverse_blocks, lower_blocks):
    block_size = inverse_blocks.shape[1]
    results = []
    earlier = None
    for counter in range(inverse_blocks.shape[0]):
        current = right_side[:, counter * block_size : (counter + 1) * block_size]
        if counter > 0:
            current = current - jnp.dot(earlier, lower_blocks[counter - 1], precision=PRECISE)
        earlier = jnp.dot(current, inverse_blocks[counter], precision=PRECISE)
        results.append(earlier)
    return jnp.concatenate(results, axis=1)


def leaf_backward(leaf_work, inverse_blocks, lower_blocks):
    block_size = inverse_blocks.shape[1]
    block_count = inverse_blocks.shape[0]
    contract_last = (((1,), (1,)), ((), ()))
    results = [None] * block_count
    later = None
    for counter in reversed(range(block_count)):
        current = leaf_work[:, counter * block_size : (counter + 1) * block_size]
        if counter < block_count - 1:
            current = current - lax.dot_general(
                later, lower_blocks[counter], contract_last, precision=PRECISE
            )
        later = lax.dot_general(current, inverse_blocks[counter], contract_last, precision=PRECISE)
        results[counter] = later
    return jnp.concatenate(results, axis=1)


def level_by_level(
    rhs_leaf,
    leaf_inv,
    leaf_sub,
    sep_rhs,
    interface,
    coupling,
    factor_one,
    factor_two,
    factor_three,
    factor_four,
    link_two,
    link_three,
    link_four,
):
    contract_last = (((1,), (1,)), ((), ()))
    gy_bits = lax.axis_size("gy").bit_length() - 1
    gx_bits = lax.axis_size("gx").bit_length() - 1
    sections = taken_lists(gy_bits, gx_bits)
    device_index = lax.axis_index(("gx", "gy"))
    factors = (factor_one[0, 0], factor_two[0, 0], factor_three[0, 0], factor_four[0, 0])
    link_mats = (link_two[0, 0], link_three[0, 0], link_four[0, 0])
    places = interface[0, 0]
    couplings = coupling[0, 0]
    own_rhs = sep_rhs[0, 0]
    inverse_blocks = leaf_inv[0, 0]
    lower_blocks = leaf_sub[0, 0]
    forward = leaf_forward(rhs_leaf[0, 0], inverse_blocks, lower_blocks)
    rhs_count = forward.shape[0]
    offsets = [0]
    for section in range(3):
        offsets.append(offsets[-1] + factors[section].shape[0])
    ranks = [rank_in_group(device_index, taken) for taken in sections]
    own_z = [None] * 4
    for section in (3, 2, 1, 0):
        own_rows, sep_width = factors[section].shape
        partials_in = lax.dot_general(forward, couplings[section], contract_last, precision=PRECISE)
        if section < 3:
            partials_in = partials_in + jnp.dot(
                own_z[section + 1], link_mats[section], precision=PRECISE
            )
        contribution = jnp.zeros((rhs_count, sep_width), jnp.float32)
        own_part = own_rhs[:, offsets[section] : offsets[section] + own_rows]
        contribution = lax.dynamic_update_slice(
            contribution, own_part, (jnp.zeros((), jnp.int32), ranks[section] * own_rows)
        )
        contribution = contribution.at[:, places[section]].add(-partials_in)
        summed = group_total(contribution, section, sections[section])
        own_z[section] = lax.dot_general(summed, factors[section], contract_last, precision=PRECISE)
    full_sep = [None] * 4
    own_x = []
    for section in range(4):
        own_rows = factors[section].shape[0]
        update = own_z[section]
        if section > 0:
            picked = full_sep[section - 1][:, places[section - 1]]
            update = update - lax.dot_general(
                picked, link_mats[section - 1], contract_last, precision=PRECISE
            )
        partial_value = jnp.dot(update, factors[section], precision=PRECISE)
        full_sep[section] = group_total(partial_value, section, sections[section])
        own_x.append(
            lax.dynamic_slice_in_dim(full_sep[section], ranks[section] * own_rows, own_rows, 1)
        )
    leaf_work = forward
    for section in range(4):
        picked = full_sep[section][:, places[section]]
        leaf_work = leaf_work - jnp.dot(picked, couplings[section], precision=PRECISE)
    leaf_solution = leaf_backward(leaf_work, inverse_blocks, lower_blocks)
    sep_solution = jnp.concatenate(own_x, axis=1)
    return (leaf_solution[None, None], sep_solution[None, None])


def halves(value):
    high = value.astype(jnp.bfloat16)
    low = (value - high.astype(jnp.float32)).astype(jnp.bfloat16)
    return high, low


def few_rows(value):
    high = value.astype(jnp.bfloat16).astype(jnp.float32)
    return jnp.concatenate([high, value - high], axis=0).astype(jnp.bfloat16)


def times(left, right, transposed):
    dims = (((1,), (1 if transposed else 0,)), ((), ()))
    stacked = few_rows(left)
    total = None
    for piece in right:
        term = lax.dot_general(stacked, piece, dims, preferred_element_type=jnp.float32)
        total = term if total is None else total + term
    rows = left.shape[0]
    return total[:rows] + total[rows:]


def wide_times(left, right):
    left = jnp.concatenate(halves(left), axis=1)
    right_high, right_low = halves(right)
    right = jnp.concatenate(
        [jnp.concatenate([right_high] * 2, axis=1), jnp.concatenate([right_low] * 2, axis=1)], axis=0
    )
    total = lax.dot_general(left, right, (((1,), (1,)), ((), ())), preferred_element_type=jnp.float32)
    width = right.shape[0] // 2
    return total[:, :width] + total[:, width:]


def one_hot(positions, height):
    rows = lax.broadcasted_iota(jnp.int32, (height, positions.shape[1]), 0)
    return (rows == positions).astype(jnp.float32).astype(jnp.bfloat16)


def wide(ref, start, rows, chunks):
    pieces = [ref[start + chunk * rows : start + (chunk + 1) * rows, :] for chunk in range(chunks)]
    return pieces[0] if chunks == 1 else jnp.concatenate(pieces, axis=1)


def vmem_call(body, outs, *operands, microseconds, after=(), space=pltpu.VMEM, scratch=(), limit=VMEM_BYTES):
    if space is pltpu.HBM:
        out_shape = [pltpu.VMEM(shape, dtype) for shape, dtype in outs]
        operands = [pltpu.with_memory_space_constraint(operand, pltpu.HBM) for operand in operands]
    else:
        out_shape = [jax.ShapeDtypeStruct(shape, dtype) for shape, dtype in outs]

    def kernel(*refs):
        body(*refs[: len(operands)], *refs[len(operands) + len(after) :])

    return pl.pallas_call(
        kernel,
        out_shape=out_shape,
        in_specs=[pl.BlockSpec(memory_space=space)] * len(operands)
        + [pl.BlockSpec(memory_space=pl.ANY)] * len(after),
        out_specs=[pl.BlockSpec(memory_space=pltpu.VMEM)] * len(outs),
        scratch_shapes=scratch,
        cost_estimate=pl.CostEstimate(
            flops=int(microseconds * FLOPS_A_MICROSECOND), bytes_accessed=0, transcendentals=0
        ),
        compiler_params=pltpu.CompilerParams(vmem_limit_bytes=limit),
    )(*operands, *after)


def packed_layout(factors, link_mats):
    starts = {}
    sets = []
    at = 0
    for section, names in enumerate((("f0",), ("f1", "l1", "places"), ("f2", "l2"), ("f3", "l3"))):
        begin = at
        for name in names:
            starts[name] = at
            if name == "places":
                at += 8
            elif name[0] == "f":
                at += factors[section].shape[0] * (factors[section].shape[1] // LANES)
            else:
                at += link_mats[section - 1].shape[0]
        sets.append((begin, at))
    return starts, tuple(sets), at


def pack_body(starts, part, f0, f1, f2, f3, l1, l2, l3, places, out, tail, s0, s1, s2, numbers, semaphores):
    moves = [(places.at[0, 0], numbers), (f0.at[0, 0], s0), (f1.at[0, 0], s1), (f2.at[0, 0], s2)]
    for name, ref in (("f3", f3), ("l1", l1), ("l2", l2), ("l3", l3)):
        moves.append((ref.at[0, 0], out.at[pl.ds(starts[name], ref.shape[2]), :]))
    copies = [
        pltpu.make_async_copy(source, target, semaphores.at[number])
        for number, (source, target) in enumerate(moves)
    ]
    for copy in copies:
        copy.start()
    for copy in copies[:4]:
        copy.wait()
    positions = numbers[...].astype(jnp.float32)
    out[starts["places"] : starts["places"] + 8, :] = jnp.concatenate([positions, positions], axis=0)
    for name, ref in (("f0", s0), ("f1", s1), ("f2", s2)):
        rows, width = ref.shape
        for chunk in range(width // LANES):
            at = starts[name] + chunk * rows
            out[at : at + rows, :] = ref[:, chunk * LANES : (chunk + 1) * LANES]
    for copy in copies[4:]:
        copy.wait()
    tail[...] = out[part[0] : part[1], :]


def own_targets(sizes, owned, taken):
    device_index = lax.axis_index("gx") * lax.axis_size("gy") + lax.axis_index("gy")
    columns = lax.broadcasted_iota(jnp.int32, (1, sum(owned)), 1)
    target = columns
    before = 0
    level_start = 0
    for section in range(4):
        rank = jnp.int32(0)
        for bit_number in sorted(taken[section], reverse=True):
            rank = rank * 2 + ((device_index >> bit_number) & 1)
        here = columns - before + (level_start + rank * owned[section])
        target = jnp.where(columns >= before, here, target)
        before += owned[section]
        level_start += sizes[section]
    return target


def forward_body(sizes, owned, taken, rhs, inverse, lower, sep_rhs, places, coupling, forward, sums):
    count, block = inverse.shape[2], inverse.shape[3]
    earlier = None
    for counter in range(count):
        current = rhs[0, 0, :, counter * block : (counter + 1) * block]
        if counter > 0:
            current = current - times(earlier, halves(lower[0, 0, counter - 1]), False)
        earlier = times(current, halves(inverse[0, 0, counter]), False)
        forward[:, counter * block : (counter + 1) * block] = earlier
    whole = forward[...]
    own = times(sep_rhs[0, 0], [one_hot(own_targets(sizes, owned, taken), sum(sizes))], True)
    terms = times(whole, halves(coupling[0, 0].reshape(-1, whole.shape[1])), True)
    width = coupling.shape[3]
    at = 0
    for section in range(4):
        term = terms[:, section * width : (section + 1) * width]
        spread = times(term, [one_hot(places[0, 0, section : section + 1, :], sizes[section])], True)
        sums[:, at : at + sizes[section]] = own[:, at : at + sizes[section]] - spread
        at += sizes[section]


def gather_body(section, starts, rows, size, above, places, *refs):
    outs = refs[len(places) :]
    at = 0
    for ref, bases in zip(refs, places):
        for base in bases:
            factor = wide(ref, base + starts["f%d" % section], rows, size // LANES)
            outs[0][at : at + rows, :], outs[1][at : at + rows, :] = halves(factor)
            if section > 0:
                place = base + starts["l%d" % section]
                link = ref[place : place + rows, :]
                row = base + starts["places"] + section - 1
                positions = ref[row : row + 1, :].astype(jnp.int32)
                linked = times(link, [one_hot(positions, above)], True)
                outs[2][at : at + rows, :], outs[3][at : at + rows, :] = halves(linked)
            at += rows


def eliminate_body(size, above, tables, mine, theirs, *refs):
    sums, found = refs[4 * tables :]
    width = mine.shape[1]
    total = mine[...] + theirs[...]
    right_side = total[:, width - size :]
    rest = total[:, width - size - above : width - size]
    at = 0
    for table in range(tables):
        f_high, f_low, m_high, m_low = refs[4 * table : 4 * table + 4]
        solved = times(right_side, [f_high[...], f_low[...]], True)
        found[:, at : at + solved.shape[1]] = solved
        rest = rest - times(solved, [m_high[...], m_low[...]], False)
        at += solved.shape[1]
    if width > size + above:
        sums[:, : width - size - above] = total[:, : width - size - above]
    sums[:, width - size - above :] = rest


def top_body(total, f_high, f_low, partial):
    pieces = [f_high[...], f_low[...]]
    partial[...] = times(times(total[...], pieces, True), pieces, False)


def join_body(moves, *refs):
    for number, start, at, rows in moves:
        refs[-1][at : at + rows, :] = refs[number][start : start + rows, :]


def copy_body(arrived, out):
    out[...] = arrived[...]


def add_body(mine, theirs, out):
    out[...] = mine[...] + theirs[...]


def fold_body(tables, found, *refs):
    solved, n_high, n_low = refs[4 * tables :]
    dims = (((0,), (0,)), ((), ()))
    known = folded = None
    at = 0
    for table in range(tables):
        f_high, f_low, m_high, m_low = refs[4 * table : 4 * table + 4]
        rows = f_high.shape[0]
        pieces = [f_high[...], f_low[...]]
        term = times(found[:, at : at + rows], pieces, False)
        known = term if known is None else known + term
        for link in (m_high[...], m_low[...]):
            for piece in pieces:
                term = lax.dot_general(link, piece, dims, preferred_element_type=jnp.float32)
                folded = term if folded is None else folded + term
        at += rows
    solved[...] = known
    n_high[...], n_low[...] = halves(folded)


def leaf_body(sections, forward, coupling, inverse, lower, base, d_high, d_low):
    count, block = inverse.shape[2], inverse.shape[3]
    rhs_count = forward.shape[0]
    rows = [coupling[0, 0, section] for section in sections]
    rows = jnp.concatenate([forward[...]] + rows, axis=0)
    later = None
    for counter in reversed(range(count)):
        current = rows[:, counter * block : (counter + 1) * block]
        if counter < count - 1:
            current = current - wide_times(later, lower[0, 0, counter])
        later = wide_times(current, inverse[0, 0, counter])
        columns = slice(counter * block, (counter + 1) * block)
        base[:, columns] = later[:rhs_count]
        d_high[:, columns], d_low[:, columns] = halves(later[rhs_count:])


def pick_body(sizes, owned, taken, places, picks, owns):
    at = 0
    for section in range(4):
        picks[at : at + sizes[section], :] = one_hot(places[0, 0, section : section + 1, :], sizes[section])
        at += sizes[section]
    owns[...] = one_hot(own_targets(sizes, owned, taken), at)


def backward_body(
    sizes, mine, theirs, u1, n1h, n1l, u2, n2h, n2l, u3, n3h, n3l, base, d1h, d1l, d2h, d2l, picks, owns, leaf, sep
):
    solved = [mine[...] + theirs[...]]
    for known, n_high, n_low in ((u1, n1h, n1l), (u2, n2h, n2l), (u3, n3h, n3l)):
        solved.append(known[...] - times(solved[-1], [n_high[...], n_low[...]], False))
    picked = []
    at = 0
    for section in range(4):
        picked.append(times(solved[section], [picks[at : at + sizes[section], :]], False))
        at += sizes[section]
    first = times(jnp.concatenate(picked[:2], axis=1), [d1h[...], d1l[...]], False)
    second = times(jnp.concatenate(picked[2:], axis=1), [d2h[...], d2l[...]], False)
    leaf[0, 0] = base[...] - first - second
    sep[0, 0] = times(jnp.concatenate(solved, axis=1), [owns[...]], False)


def gathered(
    rhs_leaf,
    leaf_inv,
    leaf_sub,
    sep_rhs,
    interface,
    coupling,
    factor_one,
    factor_two,
    factor_three,
    factor_four,
    link_two,
    link_three,
    link_four,
):
    gy_bits = lax.axis_size("gy").bit_length() - 1
    gx_bits = lax.axis_size("gx").bit_length() - 1
    taken = taken_lists(gy_bits, gx_bits)
    factors = [array.reshape(array.shape[2:]) for array in (factor_one, factor_two, factor_three, factor_four)]
    links = [array.reshape(array.shape[2:]) for array in (link_two, link_three, link_four)]
    sizes = tuple(factor.shape[1] for factor in factors)
    owned = tuple(factor.shape[0] for factor in factors)
    starts, sets, height = packed_layout(factors, links)
    axes = ("gx", "gy")
    core = gy_bits
    rhs_count = rhs_leaf.shape[2]
    total = sum(sizes)

    part = (sets[1][0], sets[2][1])
    packed, tail = vmem_call(
        functools.partial(pack_body, starts, part),
        [((height, LANES), jnp.float32), ((part[1] - part[0], LANES), jnp.float32)],
        factor_one, factor_two, factor_three, factor_four, link_two, link_three, link_four, interface,
        microseconds=1.0, space=pltpu.HBM,
        scratch=[pltpu.VMEM(factor.shape, jnp.float32) for factor in factors[:3]]
        + [pltpu.VMEM(interface.shape[2:], jnp.int32), pltpu.SemaphoreType.DMA((8,))],
    )

    everything = (0, 1, 2, 3)
    whole = ((0, everything),)
    both = [(packed, whole), (from_partner(packed, axes, core), whole)]

    def plan(wanted):
        moves, members, at = [], [], 0
        for number, (_, have) in enumerate(wanted):
            for base, its_sets, travels in have:
                first, last = sets[travels[0]][0], sets[travels[-1]][1]
                moves.append((number, base + first, at, last - first))
                members.append((at - first, travels))
                at += last - first
        return tuple(moves), tuple(members), at

    def choose(buffers, *travels):
        wanted = []
        for array, members in buffers:
            have = []
            for base, its_sets in members:
                fit = [run for run in travels if set(run) <= set(its_sets)]
                if fit:
                    have.append((base, its_sets, fit[0]))
            if have:
                wanted.append((array, tuple(have)))
        return wanted

    def message(wanted, after, microseconds=ARRIVE_US):
        moves, members, rows = plan(wanted)
        (out,) = vmem_call(
            functools.partial(join_body, moves), [((rows, LANES), jnp.float32)],
            *[array for array, _ in wanted], after=after, microseconds=microseconds,
        )
        return out, members

    def arrive(arrived, members, after, microseconds=ARRIVE_US):
        (copy,) = vmem_call(
            copy_body, [(arrived.shape, jnp.float32)], arrived, after=after, microseconds=microseconds
        )
        both.extend([(copy, members), (from_partner(copy, axes, core), members)])
        return copy, members

    def level(section, buffers, after=()):
        rows, size = factors[section].shape
        above = sizes[section - 1] if section > 0 else 0
        chosen = choose(buffers, (section,))
        places = tuple(tuple(base for base, _, _ in have) for _, have in chosen)
        count = sum(len(bases) for bases in places)
        outs = [((count * rows, size), jnp.bfloat16)] * 2
        if section > 0:
            outs = outs + [((count * rows, above), jnp.bfloat16)] * 2
        body = functools.partial(gather_body, section, starts, rows, size, above, places)
        return vmem_call(body, outs, *[array for array, _ in chosen], microseconds=TABLE_US, after=after)

    def eliminate(section, sums, theirs, tables, after):
        size, above = sizes[section], sizes[section - 1]
        flat = [array for table in tables for array in table]
        sums, found = vmem_call(
            functools.partial(eliminate_body, size, above, len(tables)),
            [((rhs_count, sums.shape[1] - size), jnp.float32), ((rhs_count, size), jnp.float32)],
            sums, theirs, *flat, microseconds=ELIM_US, after=after,
        )
        return sums, (found, *flat)

    def fold(section, pieces, after):
        size, above = sizes[section], sizes[section - 1]
        return vmem_call(
            functools.partial(fold_body, (len(pieces) - 1) // 4),
            [((rhs_count, size), jnp.float32)] + [((above, size), jnp.bfloat16)] * 2,
            *pieces, microseconds=FOLD_US, after=after,
        )

    def solve(sections, after):
        return vmem_call(
            functools.partial(leaf_body, sections),
            [((rhs_count, rhs_leaf.shape[3]), jnp.float32)]
            + [((len(sections) * LANES, rhs_leaf.shape[3]), jnp.bfloat16)] * 2,
            forward, coupling, leaf_inv, leaf_sub, microseconds=LEAF_US, after=after,
        )

    inner = min(taken[3]) if core == max(taken[3]) else max(taken[3])
    third, second, first = gy_bits + gx_bits - 2, gy_bits - 1, gy_bits + gx_bits - 1

    from_inner = from_partner(packed, axes, inner)
    from_third = from_partner(tail, axes, third)
    forward, sums = vmem_call(
        functools.partial(forward_body, sizes, owned, taken),
        [((rhs_count, rhs_leaf.shape[3]), jnp.float32), ((rhs_count, total), jnp.float32)],
        rhs_leaf, leaf_inv, leaf_sub, sep_rhs, interface, coupling, microseconds=SOLVE_US,
    )
    others = from_partner(sums, axes, core)
    by_third = arrive(from_third, ((-part[0], (1, 2)),), ())
    (sums,) = vmem_call(
        add_body, [((rhs_count, total), jnp.float32)], sums, others, microseconds=0.1, after=(by_third[0],)
    )
    theirs = from_partner(sums, axes, inner)
    by_inner = arrive(from_inner, whole, (sums,))
    following, two_at = message(choose([by_third], (1, 2)), (sums,))
    two = from_partner(following, axes, inner)
    following, near_at = message(choose([both[0], by_inner], (0, 1)), (sums,))
    near = from_partner(following, axes, second)
    table = level(3, both)
    sums, four_level = eliminate(3, sums, theirs, [table], ())

    theirs = from_partner(sums, axes, third)
    solved_first = solve((0, 1), (sums,))
    by_two = arrive(two, two_at, (solved_first[0],), X2_US)
    following, last_at = message(choose([by_third, by_two], (1,)), (sums,), Y2_US)
    by_near = arrive(near, near_at, (following,), NEAR_US)
    last = from_partner(following, axes, second)
    table = level(2, both)
    sums, three_level = eliminate(2, sums, theirs, [table], ())

    theirs = from_partner(sums, axes, second)
    following, top_at = message(choose([both[0], by_inner, by_near], (0,)), (sums,), F1_US)
    from_third = from_partner(following, axes, third)
    early = len(both)
    table = level(1, both[:early], (sums,))
    arrive(last, last_at, (table[0],), LAST_US)
    folded_three = fold(2, three_level, (sums,))
    folded_four = fold(3, four_level, (sums,))
    late = (folded_three[0], folded_four[0])
    sums, two_level = eliminate(1, sums, theirs, [table, level(1, both[early:])], late)

    theirs = from_partner(sums, axes, first)
    folded_two = fold(1, two_level, (sums,))
    arrive(from_third, top_at, (sums,), F1C_US)
    (sums,) = vmem_call(
        add_body, [((rhs_count, sizes[0]), jnp.float32)], sums, theirs, microseconds=SUM_US,
        after=(folded_two[0],),
    )
    (partial,) = vmem_call(
        top_body, [((rhs_count, sizes[0]), jnp.float32)], sums, *level(0, both, (sums,)), microseconds=0.5
    )
    theirs = from_partner(partial, axes, first)
    solved_second = solve((2, 3), (partial,))
    picks = vmem_call(
        functools.partial(pick_body, sizes, owned, taken),
        [((total, interface.shape[3]), jnp.bfloat16), ((total, sum(owned)), jnp.bfloat16)],
        interface, microseconds=0.3, after=(partial,),
    )
    leaf, sep = vmem_call(
        functools.partial(backward_body, sizes),
        [(rhs_leaf.shape, jnp.float32), (sep_rhs.shape, jnp.float32)],
        partial, theirs, *folded_two, *folded_three, *folded_four, *solved_first, *solved_second[1:], *picks,
        microseconds=2.0,
    )
    return (leaf, sep)


def local(*arrays):
    gathered_bytes = 0
    bits = lax.axis_size("gy").bit_length() + lax.axis_size("gx").bit_length() - 2
    for level, array in enumerate(arrays[6:10]):
        gathered_bytes += array.size * 4 << (bits - level)
    gy_bits = lax.axis_size("gy").bit_length() - 1
    fourth = taken_lists(gy_bits, bits - gy_bits)[3]
    if gathered_bytes > GATHER_BYTES or len(fourth) != 2 or gy_bits not in fourth:
        return level_by_level(*arrays)
    return gathered(*arrays)


def solution(mesh):
    in_specs = (
        P("gx", "gy", None, None),
        P("gx", "gy", None, None, None),
        P("gx", "gy", None, None, None),
        P("gx", "gy", None, None),
        P("gx", "gy", None, None),
        P("gx", "gy", None, None, None),
        P("gx", "gy", None, None),
        P("gx", "gy", None, None),
        P("gx", "gy", None, None),
        P("gx", "gy", None, None),
        P("gx", "gy", None, None),
        P("gx", "gy", None, None),
        P("gx", "gy", None, None),
    )
    out_specs = (P("gx", "gy", None, None), P("gx", "gy", None, None))
    return jax.shard_map(local, mesh=mesh, in_specs=in_specs, out_specs=out_specs, check_vma=False)
```

```python
import functools

import jax
import jax.numpy as jnp
from jax import lax
from jax.experimental import pallas as pl
from jax.experimental.pallas import tpu as pltpu
from jax.sharding import PartitionSpec as P

PRECISE = lax.Precision.HIGHEST
LANES = 128
GATHER_BYTES = 8 * 2**20
VMEM_BYTES = 24 * 2**20
FLOPS_A_MICROSECOND = 1_000_000_000
ARRIVE_US = 0.1
SOLVE_US = 2.0
X2_US = 5.0
NEAR_US = 5.0
Y2_US = 5.0
LAST_US = 0.1
F1_US = 5.0
F1C_US = 0.1
SUM_US = 5.0
TABLE_US = 0.4
FOLD_US = 0.5
LEAF_US = 1.0
ELIM_US = 5.0


def from_partner(value, axis, distance):
    return lax.ppermute(value, axis, [(i, i ^ 1 << distance) for i in range(lax.axis_size(axis))])


def taken_lists(gy_bits, gx_bits):
    first = list(range(gy_bits + gx_bits))
    second = [bit_number for bit_number in first if bit_number != gy_bits + gx_bits - 1]
    third = [bit_number for bit_number in second if bit_number != gy_bits - 1]
    fourth = [bit_number for bit_number in third if bit_number != gy_bits + gx_bits - 2]
    return [first, second, third, fourth]


def rank_in_group(device_index, taken):
    group_rank = jnp.zeros((), jnp.int32)
    for bit_number in sorted(taken, reverse=True):
        group_rank = group_rank * 2 + (device_index >> bit_number & 1)
    return group_rank


def group_total(values, section, taken):
    if section == 0:
        return lax.psum(values, ("gx", "gy"))
    for bit_number in sorted(taken, reverse=True):
        values = values + from_partner(values, ("gx", "gy"), bit_number)
    return values


def leaf_forward(right_side, inverse_blocks, lower_blocks):
    block_size = inverse_blocks.shape[1]
    results = []
    earlier = None
    for counter in range(inverse_blocks.shape[0]):
        current = right_side[:, counter * block_size : (counter + 1) * block_size]
        if counter > 0:
            current = current - jnp.dot(earlier, lower_blocks[counter - 1], precision=PRECISE)
        earlier = jnp.dot(current, inverse_blocks[counter], precision=PRECISE)
        results.append(earlier)
    return jnp.concatenate(results, axis=1)


def leaf_backward(leaf_work, inverse_blocks, lower_blocks):
    block_size = inverse_blocks.shape[1]
    block_count = inverse_blocks.shape[0]
    contract_last = (((1,), (1,)), ((), ()))
    results = [None] * block_count
    later = None
    for counter in reversed(range(block_count)):
        current = leaf_work[:, counter * block_size : (counter + 1) * block_size]
        if counter < block_count - 1:
            current = current - lax.dot_general(
                later, lower_blocks[counter], contract_last, precision=PRECISE
            )
        later = lax.dot_general(current, inverse_blocks[counter], contract_last, precision=PRECISE)
        results[counter] = later
    return jnp.concatenate(results, axis=1)


def level_by_level(
    rhs_leaf,
    leaf_inv,
    leaf_sub,
    sep_rhs,
    interface,
    coupling,
    factor_one,
    factor_two,
    factor_three,
    factor_four,
    link_two,
    link_three,
    link_four,
):
    contract_last = (((1,), (1,)), ((), ()))
    gy_bits = lax.axis_size("gy").bit_length() - 1
    gx_bits = lax.axis_size("gx").bit_length() - 1
    sections = taken_lists(gy_bits, gx_bits)
    device_index = lax.axis_index(("gx", "gy"))
    factors = (factor_one[0, 0], factor_two[0, 0], factor_three[0, 0], factor_four[0, 0])
    link_mats = (link_two[0, 0], link_three[0, 0], link_four[0, 0])
    places = interface[0, 0]
    couplings = coupling[0, 0]
    own_rhs = sep_rhs[0, 0]
    inverse_blocks = leaf_inv[0, 0]
    lower_blocks = leaf_sub[0, 0]
    forward = leaf_forward(rhs_leaf[0, 0], inverse_blocks, lower_blocks)
    rhs_count = forward.shape[0]
    offsets = [0]
    for section in range(3):
        offsets.append(offsets[-1] + factors[section].shape[0])
    ranks = [rank_in_group(device_index, taken) for taken in sections]
    own_z = [None] * 4
    for section in (3, 2, 1, 0):
        own_rows, sep_width = factors[section].shape
        partials_in = lax.dot_general(forward, couplings[section], contract_last, precision=PRECISE)
        if section < 3:
            partials_in = partials_in + jnp.dot(
                own_z[section + 1], link_mats[section], precision=PRECISE
            )
        contribution = jnp.zeros((rhs_count, sep_width), jnp.float32)
        own_part = own_rhs[:, offsets[section] : offsets[section] + own_rows]
        contribution = lax.dynamic_update_slice(
            contribution, own_part, (jnp.zeros((), jnp.int32), ranks[section] * own_rows)
        )
        contribution = contribution.at[:, places[section]].add(-partials_in)
        summed = group_total(contribution, section, sections[section])
        own_z[section] = lax.dot_general(summed, factors[section], contract_last, precision=PRECISE)
    full_sep = [None] * 4
    own_x = []
    for section in range(4):
        own_rows = factors[section].shape[0]
        update = own_z[section]
        if section > 0:
            picked = full_sep[section - 1][:, places[section - 1]]
            update = update - lax.dot_general(
                picked, link_mats[section - 1], contract_last, precision=PRECISE
            )
        partial_value = jnp.dot(update, factors[section], precision=PRECISE)
        full_sep[section] = group_total(partial_value, section, sections[section])
        own_x.append(
            lax.dynamic_slice_in_dim(full_sep[section], ranks[section] * own_rows, own_rows, 1)
        )
    leaf_work = forward
    for section in range(4):
        picked = full_sep[section][:, places[section]]
        leaf_work = leaf_work - jnp.dot(picked, couplings[section], precision=PRECISE)
    leaf_solution = leaf_backward(leaf_work, inverse_blocks, lower_blocks)
    sep_solution = jnp.concatenate(own_x, axis=1)
    return (leaf_solution[None, None], sep_solution[None, None])


def halves(value):
    high = value.astype(jnp.bfloat16)
    low = (value - high.astype(jnp.float32)).astype(jnp.bfloat16)
    return high, low


def few_rows(value):
    high = value.astype(jnp.bfloat16).astype(jnp.float32)
    return jnp.concatenate([high, value - high], axis=0).astype(jnp.bfloat16)


def times(left, right, transposed):
    dims = (((1,), (1 if transposed else 0,)), ((), ()))
    stacked = few_rows(left)
    total = None
    for piece in right:
        term = lax.dot_general(stacked, piece, dims, preferred_element_type=jnp.float32)
        total = term if total is None else total + term
    rows = left.shape[0]
    return total[:rows] + total[rows:]


def wide_times(left, right):
    left = jnp.concatenate(halves(left), axis=1)
    right_high, right_low = halves(right)
    right = jnp.concatenate(
        [jnp.concatenate([right_high] * 2, axis=1), jnp.concatenate([right_low] * 2, axis=1)], axis=0
    )
    total = lax.dot_general(left, right, (((1,), (1,)), ((), ())), preferred_element_type=jnp.float32)
    width = right.shape[0] // 2
    return total[:, :width] + total[:, width:]


def one_hot(positions, height):
    rows = lax.broadcasted_iota(jnp.int32, (height, positions.shape[1]), 0)
    return (rows == positions).astype(jnp.float32).astype(jnp.bfloat16)


def wide(ref, start, rows, chunks):
    pieces = [ref[start + chunk * rows : start + (chunk + 1) * rows, :] for chunk in range(chunks)]
    return pieces[0] if chunks == 1 else jnp.concatenate(pieces, axis=1)


def vmem_call(body, outs, *operands, microseconds, after=(), space=pltpu.VMEM, scratch=(), limit=VMEM_BYTES):
    if space is pltpu.HBM:
        out_shape = [pltpu.VMEM(shape, dtype) for shape, dtype in outs]
        operands = [pltpu.with_memory_space_constraint(operand, pltpu.HBM) for operand in operands]
    else:
        out_shape = [jax.ShapeDtypeStruct(shape, dtype) for shape, dtype in outs]

    def kernel(*refs):
        body(*refs[: len(operands)], *refs[len(operands) + len(after) :])

    return pl.pallas_call(
        kernel,
        out_shape=out_shape,
        in_specs=[pl.BlockSpec(memory_space=space)] * len(operands)
        + [pl.BlockSpec(memory_space=pl.ANY)] * len(after),
        out_specs=[pl.BlockSpec(memory_space=pltpu.VMEM)] * len(outs),
        scratch_shapes=scratch,
        cost_estimate=pl.CostEstimate(
            flops=int(microseconds * FLOPS_A_MICROSECOND), bytes_accessed=0, transcendentals=0
        ),
        compiler_params=pltpu.CompilerParams(vmem_limit_bytes=limit),
    )(*operands, *after)


def packed_layout(factors, link_mats):
    starts = {}
    sets = []
    at = 0
    for section, names in enumerate((("f0",), ("f1", "l1", "places"), ("f2", "l2"), ("f3", "l3"))):
        begin = at
        for name in names:
            starts[name] = at
            if name == "places":
                at += 8
            elif name[0] == "f":
                at += factors[section].shape[0] * (factors[section].shape[1] // LANES)
            else:
                at += link_mats[section - 1].shape[0]
        sets.append((begin, at))
    return starts, tuple(sets), at


def pack_body(starts, part, f0, f1, f2, f3, l1, l2, l3, places, out, tail, s0, s1, s2, numbers, semaphores):
    moves = [(places.at[0, 0], numbers), (f0.at[0, 0], s0), (f1.at[0, 0], s1), (f2.at[0, 0], s2)]
    for name, ref in (("f3", f3), ("l1", l1), ("l2", l2), ("l3", l3)):
        moves.append((ref.at[0, 0], out.at[pl.ds(starts[name], ref.shape[2]), :]))
    copies = [
        pltpu.make_async_copy(source, target, semaphores.at[number])
        for number, (source, target) in enumerate(moves)
    ]
    for copy in copies:
        copy.start()
    for copy in copies[:4]:
        copy.wait()
    positions = numbers[...].astype(jnp.float32)
    out[starts["places"] : starts["places"] + 8, :] = jnp.concatenate([positions, positions], axis=0)
    for name, ref in (("f0", s0), ("f1", s1), ("f2", s2)):
        rows, width = ref.shape
        for chunk in range(width // LANES):
            at = starts[name] + chunk * rows
            out[at : at + rows, :] = ref[:, chunk * LANES : (chunk + 1) * LANES]
    for copy in copies[4:]:
        copy.wait()
    tail[...] = out[part[0] : part[1], :]


def own_targets(sizes, owned, taken):
    device_index = lax.axis_index("gx") * lax.axis_size("gy") + lax.axis_index("gy")
    columns = lax.broadcasted_iota(jnp.int32, (1, sum(owned)), 1)
    target = columns
    before = 0
    level_start = 0
    for section in range(4):
        rank = jnp.int32(0)
        for bit_number in sorted(taken[section], reverse=True):
            rank = rank * 2 + ((device_index >> bit_number) & 1)
        here = columns - before + (level_start + rank * owned[section])
        target = jnp.where(columns >= before, here, target)
        before += owned[section]
        level_start += sizes[section]
    return target


def forward_body(sizes, owned, taken, rhs, inverse, lower, sep_rhs, places, coupling, forward, sums):
    count, block = inverse.shape[2], inverse.shape[3]
    earlier = None
    for counter in range(count):
        current = rhs[0, 0, :, counter * block : (counter + 1) * block]
        if counter > 0:
            current = current - times(earlier, halves(lower[0, 0, counter - 1]), False)
        earlier = times(current, halves(inverse[0, 0, counter]), False)
        forward[:, counter * block : (counter + 1) * block] = earlier
    whole = forward[...]
    own = times(sep_rhs[0, 0], [one_hot(own_targets(sizes, owned, taken), sum(sizes))], True)
    terms = times(whole, halves(coupling[0, 0].reshape(-1, whole.shape[1])), True)
    width = coupling.shape[3]
    at = 0
    for section in range(4):
        term = terms[:, section * width : (section + 1) * width]
        spread = times(term, [one_hot(places[0, 0, section : section + 1, :], sizes[section])], True)
        sums[:, at : at + sizes[section]] = own[:, at : at + sizes[section]] - spread
        at += sizes[section]


def gather_body(section, starts, rows, size, above, places, *refs):
    outs = refs[len(places) :]
    at = 0
    for ref, bases in zip(refs, places):
        for base in bases:
            factor = wide(ref, base + starts["f%d" % section], rows, size // LANES)
            outs[0][at : at + rows, :], outs[1][at : at + rows, :] = halves(factor)
            if section > 0:
                place = base + starts["l%d" % section]
                link = ref[place : place + rows, :]
                row = base + starts["places"] + section - 1
                positions = ref[row : row + 1, :].astype(jnp.int32)
                linked = times(link, [one_hot(positions, above)], True)
                outs[2][at : at + rows, :], outs[3][at : at + rows, :] = halves(linked)
            at += rows


def eliminate_body(size, above, tables, mine, theirs, *refs):
    sums, found = refs[4 * tables :]
    width = mine.shape[1]
    total = mine[...] + theirs[...]
    right_side = total[:, width - size :]
    rest = total[:, width - size - above : width - size]
    at = 0
    for table in range(tables):
        f_high, f_low, m_high, m_low = refs[4 * table : 4 * table + 4]
        solved = times(right_side, [f_high[...], f_low[...]], True)
        found[:, at : at + solved.shape[1]] = solved
        rest = rest - times(solved, [m_high[...], m_low[...]], False)
        at += solved.shape[1]
    if width > size + above:
        sums[:, : width - size - above] = total[:, : width - size - above]
    sums[:, width - size - above :] = rest


def top_body(total, f_high, f_low, partial):
    pieces = [f_high[...], f_low[...]]
    partial[...] = times(times(total[...], pieces, True), pieces, False)


def join_body(moves, *refs):
    for number, start, at, rows in moves:
        refs[-1][at : at + rows, :] = refs[number][start : start + rows, :]


def copy_body(arrived, out):
    out[...] = arrived[...]


def add_body(mine, theirs, out):
    out[...] = mine[...] + theirs[...]


def fold_body(tables, found, *refs):
    solved, n_high, n_low = refs[4 * tables :]
    dims = (((0,), (0,)), ((), ()))
    known = folded = None
    at = 0
    for table in range(tables):
        f_high, f_low, m_high, m_low = refs[4 * table : 4 * table + 4]
        rows = f_high.shape[0]
        pieces = [f_high[...], f_low[...]]
        term = times(found[:, at : at + rows], pieces, False)
        known = term if known is None else known + term
        for link in (m_high[...], m_low[...]):
            for piece in pieces:
                term = lax.dot_general(link, piece, dims, preferred_element_type=jnp.float32)
                folded = term if folded is None else folded + term
        at += rows
    solved[...] = known
    n_high[...], n_low[...] = halves(folded)


def leaf_body(sections, forward, coupling, inverse, lower, *outs):
    count, block = inverse.shape[2], inverse.shape[3]
    d_high, d_low = outs[-2:]
    rows = [coupling[0, 0, section] for section in sections]
    if len(outs) == 3:
        rows = [forward[...]] + rows
    rows = jnp.concatenate(rows, axis=0)
    first = rows.shape[0] - d_high.shape[0]
    later = None
    for counter in reversed(range(count)):
        current = rows[:, counter * block : (counter + 1) * block]
        if counter < count - 1:
            current = current - wide_times(later, lower[0, 0, counter])
        later = wide_times(current, inverse[0, 0, counter])
        columns = slice(counter * block, (counter + 1) * block)
        if first:
            outs[0][:, columns] = later[:first]
        d_high[:, columns], d_low[:, columns] = halves(later[first:])


def pick_body(sizes, owned, taken, places, picks, owns):
    at = 0
    for section in range(4):
        picks[at : at + sizes[section], :] = one_hot(places[0, 0, section : section + 1, :], sizes[section])
        at += sizes[section]
    owns[...] = one_hot(own_targets(sizes, owned, taken), at)


def backward_body(
    sizes, mine, theirs, u1, n1h, n1l, u2, n2h, n2l, u3, n3h, n3l, base, d1h, d1l, d2h, d2l, picks, owns, leaf, sep
):
    starts = [sum(sizes[:section]) for section in range(4)]

    def pick(section):
        return times(solved[section], [picks[starts[section] : starts[section] + sizes[section], :]], False)

    solved = [mine[...] + theirs[...]]
    solved.append(u1[...] - times(solved[0], [n1h[...], n1l[...]], False))
    picked = [pick(0)]
    solved.append(u2[...] - times(solved[1], [n2h[...], n2l[...]], False))
    picked.append(pick(1))
    solved.append(u3[...] - times(solved[2], [n3h[...], n3l[...]], False))
    first = base[...] - times(jnp.concatenate(picked, axis=1), [d1h[...], d1l[...]], False)
    owned = times(jnp.concatenate(solved[:3], axis=1), [owns[: starts[3], :]], False)
    picked = jnp.concatenate([pick(2), pick(3)], axis=1)
    leaf[0, 0] = first - times(picked, [d2h[...], d2l[...]], False)
    sep[0, 0] = owned + times(solved[3], [owns[starts[3] :, :]], False)


def gathered(
    rhs_leaf,
    leaf_inv,
    leaf_sub,
    sep_rhs,
    interface,
    coupling,
    factor_one,
    factor_two,
    factor_three,
    factor_four,
    link_two,
    link_three,
    link_four,
):
    gy_bits = lax.axis_size("gy").bit_length() - 1
    gx_bits = lax.axis_size("gx").bit_length() - 1
    taken = taken_lists(gy_bits, gx_bits)
    factors = [array.reshape(array.shape[2:]) for array in (factor_one, factor_two, factor_three, factor_four)]
    links = [array.reshape(array.shape[2:]) for array in (link_two, link_three, link_four)]
    sizes = tuple(factor.shape[1] for factor in factors)
    owned = tuple(factor.shape[0] for factor in factors)
    starts, sets, height = packed_layout(factors, links)
    axes = ("gx", "gy")
    core = gy_bits
    rhs_count = rhs_leaf.shape[2]
    total = sum(sizes)

    part = (sets[1][0], sets[2][1])
    packed, tail = vmem_call(
        functools.partial(pack_body, starts, part),
        [((height, LANES), jnp.float32), ((part[1] - part[0], LANES), jnp.float32)],
        factor_one, factor_two, factor_three, factor_four, link_two, link_three, link_four, interface,
        microseconds=1.0, space=pltpu.HBM,
        scratch=[pltpu.VMEM(factor.shape, jnp.float32) for factor in factors[:3]]
        + [pltpu.VMEM(interface.shape[2:], jnp.int32), pltpu.SemaphoreType.DMA((8,))],
    )

    everything = (0, 1, 2, 3)
    whole = ((0, everything),)
    both = [(packed, whole), (from_partner(packed, axes, core), whole)]

    def plan(wanted):
        moves, members, at = [], [], 0
        for number, (_, have) in enumerate(wanted):
            for base, its_sets, travels in have:
                first, last = sets[travels[0]][0], sets[travels[-1]][1]
                moves.append((number, base + first, at, last - first))
                members.append((at - first, travels))
                at += last - first
        return tuple(moves), tuple(members), at

    def choose(buffers, *travels):
        wanted = []
        for array, members in buffers:
            have = []
            for base, its_sets in members:
                fit = [run for run in travels if set(run) <= set(its_sets)]
                if fit:
                    have.append((base, its_sets, fit[0]))
            if have:
                wanted.append((array, tuple(have)))
        return wanted

    def message(wanted, after, microseconds=ARRIVE_US):
        moves, members, rows = plan(wanted)
        (out,) = vmem_call(
            functools.partial(join_body, moves), [((rows, LANES), jnp.float32)],
            *[array for array, _ in wanted], after=after, microseconds=microseconds,
        )
        return out, members

    def arrive(arrived, members, after, microseconds=ARRIVE_US):
        (copy,) = vmem_call(
            copy_body, [(arrived.shape, jnp.float32)], arrived, after=after, microseconds=microseconds
        )
        both.extend([(copy, members), (from_partner(copy, axes, core), members)])
        return copy, members

    def level(section, buffers, after=()):
        rows, size = factors[section].shape
        above = sizes[section - 1] if section > 0 else 0
        chosen = choose(buffers, (section,))
        places = tuple(tuple(base for base, _, _ in have) for _, have in chosen)
        count = sum(len(bases) for bases in places)
        outs = [((count * rows, size), jnp.bfloat16)] * 2
        if section > 0:
            outs = outs + [((count * rows, above), jnp.bfloat16)] * 2
        body = functools.partial(gather_body, section, starts, rows, size, above, places)
        return vmem_call(body, outs, *[array for array, _ in chosen], microseconds=TABLE_US, after=after)

    def eliminate(section, sums, theirs, tables, after):
        size, above = sizes[section], sizes[section - 1]
        flat = [array for table in tables for array in table]
        sums, found = vmem_call(
            functools.partial(eliminate_body, size, above, len(tables)),
            [((rhs_count, sums.shape[1] - size), jnp.float32), ((rhs_count, size), jnp.float32)],
            sums, theirs, *flat, microseconds=ELIM_US, after=after,
        )
        return sums, (found, *flat)

    def fold(section, pieces, after):
        size, above = sizes[section], sizes[section - 1]
        return vmem_call(
            functools.partial(fold_body, (len(pieces) - 1) // 4),
            [((rhs_count, size), jnp.float32)] + [((above, size), jnp.bfloat16)] * 2,
            *pieces, microseconds=FOLD_US, after=after,
        )

    def solve(sections, with_forward, after):
        rows = len(sections) * LANES
        return vmem_call(
            functools.partial(leaf_body, sections),
            [((rhs_count, rhs_leaf.shape[3]), jnp.float32)] * with_forward
            + [((rows, rhs_leaf.shape[3]), jnp.bfloat16)] * 2,
            forward, coupling, leaf_inv, leaf_sub, microseconds=LEAF_US, after=after,
        )

    inner = min(taken[3]) if core == max(taken[3]) else max(taken[3])
    third, second, first = gy_bits + gx_bits - 2, gy_bits - 1, gy_bits + gx_bits - 1

    from_inner = from_partner(packed, axes, inner)
    from_third = from_partner(tail, axes, third)
    forward, sums = vmem_call(
        functools.partial(forward_body, sizes, owned, taken),
        [((rhs_count, rhs_leaf.shape[3]), jnp.float32), ((rhs_count, total), jnp.float32)],
        rhs_leaf, leaf_inv, leaf_sub, sep_rhs, interface, coupling, microseconds=SOLVE_US,
    )
    others = from_partner(sums, axes, core)
    by_third = arrive(from_third, ((-part[0], (1, 2)),), ())
    (sums,) = vmem_call(
        add_body, [((rhs_count, total), jnp.float32)], sums, others, microseconds=0.1, after=(by_third[0],)
    )
    theirs = from_partner(sums, axes, inner)
    by_inner = arrive(from_inner, whole, (sums,))
    following, two_at = message(choose([by_third], (1, 2)), (sums,))
    two = from_partner(following, axes, inner)
    following, near_at = message(choose([both[0], by_inner], (0, 1)), (sums,))
    near = from_partner(following, axes, second)
    table = level(3, both)
    sums, four_level = eliminate(3, sums, theirs, [table], ())

    theirs = from_partner(sums, axes, third)
    solved_first = solve((0, 1), True, (sums,))
    by_two = arrive(two, two_at, (solved_first[0],), X2_US)
    following, last_at = message(choose([by_third, by_two], (1,)), (sums,), Y2_US)
    by_near = arrive(near, near_at, (following,), NEAR_US)
    last = from_partner(following, axes, second)
    table = level(2, both)
    sums, three_level = eliminate(2, sums, theirs, [table], ())

    theirs = from_partner(sums, axes, second)
    following, top_at = message(choose([both[0], by_inner, by_near], (0,)), (sums,), F1_US)
    from_third = from_partner(following, axes, third)
    early = len(both)
    table = level(1, both[:early], (sums,))
    arrive(last, last_at, (table[0],), LAST_US)
    folded_three = fold(2, three_level, (sums,))
    late = (folded_three[0],)
    sums, two_level = eliminate(1, sums, theirs, [table, level(1, both[early:])], late)

    theirs = from_partner(sums, axes, first)
    folded_two = fold(1, two_level, (sums,))
    arrive(from_third, top_at, (sums,), F1C_US)
    (sums,) = vmem_call(
        add_body, [((rhs_count, sizes[0]), jnp.float32)], sums, theirs, microseconds=SUM_US,
        after=(folded_two[0],),
    )
    (partial,) = vmem_call(
        top_body, [((rhs_count, sizes[0]), jnp.float32)], sums, *level(0, both, (sums,)), microseconds=0.5
    )
    theirs = from_partner(partial, axes, first)
    solved_second = solve((2, 3), False, (partial,))
    folded_four = fold(3, four_level, (partial,))
    picks = vmem_call(
        functools.partial(pick_body, sizes, owned, taken),
        [((total, interface.shape[3]), jnp.bfloat16), ((total, sum(owned)), jnp.bfloat16)],
        interface, microseconds=0.3, after=(partial,),
    )
    leaf, sep = vmem_call(
        functools.partial(backward_body, sizes),
        [(rhs_leaf.shape, jnp.float32), (sep_rhs.shape, jnp.float32)],
        partial, theirs, *folded_two, *folded_three, *folded_four, *solved_first, *solved_second, *picks,
        microseconds=2.0,
    )
    return (leaf, sep)


def local(*arrays):
    gathered_bytes = 0
    bits = lax.axis_size("gy").bit_length() + lax.axis_size("gx").bit_length() - 2
    for level, array in enumerate(arrays[6:10]):
        gathered_bytes += array.size * 4 << (bits - level)
    gy_bits = lax.axis_size("gy").bit_length() - 1
    fourth = taken_lists(gy_bits, bits - gy_bits)[3]
    if gathered_bytes > GATHER_BYTES or len(fourth) != 2 or gy_bits not in fourth:
        return level_by_level(*arrays)
    return gathered(*arrays)


def solution(mesh):
    in_specs = (
        P("gx", "gy", None, None),
        P("gx", "gy", None, None, None),
        P("gx", "gy", None, None, None),
        P("gx", "gy", None, None),
        P("gx", "gy", None, None),
        P("gx", "gy", None, None, None),
        P("gx", "gy", None, None),
        P("gx", "gy", None, None),
        P("gx", "gy", None, None),
        P("gx", "gy", None, None),
        P("gx", "gy", None, None),
        P("gx", "gy", None, None),
        P("gx", "gy", None, None),
    )
    out_specs = (P("gx", "gy", None, None), P("gx", "gy", None, None))
    return jax.shard_map(local, mesh=mesh, in_specs=in_specs, out_specs=out_specs, check_vma=False)
```

```python
import functools

import jax
import jax.numpy as jnp
from jax import lax
from jax.experimental import pallas as pl
from jax.experimental.pallas import tpu as pltpu
from jax.sharding import PartitionSpec as P

PRECISE = lax.Precision.HIGHEST
LANES = 128
GATHER_BYTES = 8 * 2**20
VMEM_BYTES = 24 * 2**20
FLOPS_A_MICROSECOND = 1_000_000_000
ARRIVE_US = 0.1
SOLVE_US = 2.0
X2_US = 5.0
NEAR_US = 5.0
Y2_US = 5.0
LAST_US = 0.1
F1_US = 5.0
F1C_US = 0.1
SUM_US = 5.0
TABLE_US = 0.4
FOLD_US = 0.5
LEAF_US = 1.0
ELIM_US = 5.0


def from_partner(value, axis, distance):
    return lax.ppermute(value, axis, [(i, i ^ 1 << distance) for i in range(lax.axis_size(axis))])


def taken_lists(gy_bits, gx_bits):
    first = list(range(gy_bits + gx_bits))
    second = [bit_number for bit_number in first if bit_number != gy_bits + gx_bits - 1]
    third = [bit_number for bit_number in second if bit_number != gy_bits - 1]
    fourth = [bit_number for bit_number in third if bit_number != gy_bits + gx_bits - 2]
    return [first, second, third, fourth]


def rank_in_group(device_index, taken):
    group_rank = jnp.zeros((), jnp.int32)
    for bit_number in sorted(taken, reverse=True):
        group_rank = group_rank * 2 + (device_index >> bit_number & 1)
    return group_rank


def group_total(values, section, taken):
    if section == 0:
        return lax.psum(values, ("gx", "gy"))
    for bit_number in sorted(taken, reverse=True):
        values = values + from_partner(values, ("gx", "gy"), bit_number)
    return values


def leaf_forward(right_side, inverse_blocks, lower_blocks):
    block_size = inverse_blocks.shape[1]
    results = []
    earlier = None
    for counter in range(inverse_blocks.shape[0]):
        current = right_side[:, counter * block_size : (counter + 1) * block_size]
        if counter > 0:
            current = current - jnp.dot(earlier, lower_blocks[counter - 1], precision=PRECISE)
        earlier = jnp.dot(current, inverse_blocks[counter], precision=PRECISE)
        results.append(earlier)
    return jnp.concatenate(results, axis=1)


def leaf_backward(leaf_work, inverse_blocks, lower_blocks):
    block_size = inverse_blocks.shape[1]
    block_count = inverse_blocks.shape[0]
    contract_last = (((1,), (1,)), ((), ()))
    results = [None] * block_count
    later = None
    for counter in reversed(range(block_count)):
        current = leaf_work[:, counter * block_size : (counter + 1) * block_size]
        if counter < block_count - 1:
            current = current - lax.dot_general(
                later, lower_blocks[counter], contract_last, precision=PRECISE
            )
        later = lax.dot_general(current, inverse_blocks[counter], contract_last, precision=PRECISE)
        results[counter] = later
    return jnp.concatenate(results, axis=1)


def level_by_level(
    rhs_leaf,
    leaf_inv,
    leaf_sub,
    sep_rhs,
    interface,
    coupling,
    factor_one,
    factor_two,
    factor_three,
    factor_four,
    link_two,
    link_three,
    link_four,
):
    contract_last = (((1,), (1,)), ((), ()))
    gy_bits = lax.axis_size("gy").bit_length() - 1
    gx_bits = lax.axis_size("gx").bit_length() - 1
    sections = taken_lists(gy_bits, gx_bits)
    device_index = lax.axis_index(("gx", "gy"))
    factors = (factor_one[0, 0], factor_two[0, 0], factor_three[0, 0], factor_four[0, 0])
    link_mats = (link_two[0, 0], link_three[0, 0], link_four[0, 0])
    places = interface[0, 0]
    couplings = coupling[0, 0]
    own_rhs = sep_rhs[0, 0]
    inverse_blocks = leaf_inv[0, 0]
    lower_blocks = leaf_sub[0, 0]
    forward = leaf_forward(rhs_leaf[0, 0], inverse_blocks, lower_blocks)
    rhs_count = forward.shape[0]
    offsets = [0]
    for section in range(3):
        offsets.append(offsets[-1] + factors[section].shape[0])
    ranks = [rank_in_group(device_index, taken) for taken in sections]
    own_z = [None] * 4
    for section in (3, 2, 1, 0):
        own_rows, sep_width = factors[section].shape
        partials_in = lax.dot_general(forward, couplings[section], contract_last, precision=PRECISE)
        if section < 3:
            partials_in = partials_in + jnp.dot(
                own_z[section + 1], link_mats[section], precision=PRECISE
            )
        contribution = jnp.zeros((rhs_count, sep_width), jnp.float32)
        own_part = own_rhs[:, offsets[section] : offsets[section] + own_rows]
        contribution = lax.dynamic_update_slice(
            contribution, own_part, (jnp.zeros((), jnp.int32), ranks[section] * own_rows)
        )
        contribution = contribution.at[:, places[section]].add(-partials_in)
        summed = group_total(contribution, section, sections[section])
        own_z[section] = lax.dot_general(summed, factors[section], contract_last, precision=PRECISE)
    full_sep = [None] * 4
    own_x = []
    for section in range(4):
        own_rows = factors[section].shape[0]
        update = own_z[section]
        if section > 0:
            picked = full_sep[section - 1][:, places[section - 1]]
            update = update - lax.dot_general(
                picked, link_mats[section - 1], contract_last, precision=PRECISE
            )
        partial_value = jnp.dot(update, factors[section], precision=PRECISE)
        full_sep[section] = group_total(partial_value, section, sections[section])
        own_x.append(
            lax.dynamic_slice_in_dim(full_sep[section], ranks[section] * own_rows, own_rows, 1)
        )
    leaf_work = forward
    for section in range(4):
        picked = full_sep[section][:, places[section]]
        leaf_work = leaf_work - jnp.dot(picked, couplings[section], precision=PRECISE)
    leaf_solution = leaf_backward(leaf_work, inverse_blocks, lower_blocks)
    sep_solution = jnp.concatenate(own_x, axis=1)
    return (leaf_solution[None, None], sep_solution[None, None])


def halves(value):
    high = value.astype(jnp.bfloat16)
    low = (value - high.astype(jnp.float32)).astype(jnp.bfloat16)
    return high, low


def few_rows(value):
    high = value.astype(jnp.bfloat16).astype(jnp.float32)
    return jnp.concatenate([high, value - high], axis=0).astype(jnp.bfloat16)


def times(left, right, transposed):
    dims = (((1,), (1 if transposed else 0,)), ((), ()))
    stacked = few_rows(left)
    total = None
    for piece in right:
        term = lax.dot_general(stacked, piece, dims, preferred_element_type=jnp.float32)
        total = term if total is None else total + term
    rows = left.shape[0]
    return total[:rows] + total[rows:]


def wide_times(left, right):
    left = jnp.concatenate(halves(left), axis=1)
    right_high, right_low = halves(right)
    right = jnp.concatenate(
        [jnp.concatenate([right_high] * 2, axis=1), jnp.concatenate([right_low] * 2, axis=1)], axis=0
    )
    total = lax.dot_general(left, right, (((1,), (1,)), ((), ())), preferred_element_type=jnp.float32)
    width = right.shape[0] // 2
    return total[:, :width] + total[:, width:]


def one_hot(positions, height):
    rows = lax.broadcasted_iota(jnp.int32, (height, positions.shape[1]), 0)
    return (rows == positions).astype(jnp.float32).astype(jnp.bfloat16)


def wide(ref, start, rows, chunks):
    pieces = [ref[start + chunk * rows : start + (chunk + 1) * rows, :] for chunk in range(chunks)]
    return pieces[0] if chunks == 1 else jnp.concatenate(pieces, axis=1)


def vmem_call(body, outs, *operands, microseconds, after=(), space=pltpu.VMEM, scratch=(), limit=VMEM_BYTES):
    if space is pltpu.HBM:
        out_shape = [pltpu.VMEM(shape, dtype) for shape, dtype in outs]
        operands = [pltpu.with_memory_space_constraint(operand, pltpu.HBM) for operand in operands]
    else:
        out_shape = [jax.ShapeDtypeStruct(shape, dtype) for shape, dtype in outs]

    def kernel(*refs):
        body(*refs[: len(operands)], *refs[len(operands) + len(after) :])

    return pl.pallas_call(
        kernel,
        out_shape=out_shape,
        in_specs=[pl.BlockSpec(memory_space=space)] * len(operands)
        + [pl.BlockSpec(memory_space=pl.ANY)] * len(after),
        out_specs=[pl.BlockSpec(memory_space=pltpu.VMEM)] * len(outs),
        scratch_shapes=scratch,
        cost_estimate=pl.CostEstimate(
            flops=int(microseconds * FLOPS_A_MICROSECOND), bytes_accessed=0, transcendentals=0
        ),
        compiler_params=pltpu.CompilerParams(vmem_limit_bytes=limit),
    )(*operands, *after)


def packed_layout(factors, link_mats):
    starts = {}
    sets = []
    at = 0
    for section, names in enumerate((("f0",), ("f1", "l1", "places"), ("f2", "l2"), ("f3", "l3"))):
        begin = at
        for name in names:
            starts[name] = at
            if name == "places":
                at += 8
            elif name[0] == "f":
                at += factors[section].shape[0] * (factors[section].shape[1] // LANES)
            else:
                at += link_mats[section - 1].shape[0]
        sets.append((begin, at))
    return starts, tuple(sets), at


def pack_body(starts, part, f0, f1, f2, f3, l1, l2, l3, places, out, tail, s0, s1, s2, numbers, semaphores):
    moves = [(places.at[0, 0], numbers), (f0.at[0, 0], s0), (f1.at[0, 0], s1), (f2.at[0, 0], s2)]
    for name, ref in (("f3", f3), ("l1", l1), ("l2", l2), ("l3", l3)):
        moves.append((ref.at[0, 0], out.at[pl.ds(starts[name], ref.shape[2]), :]))
    copies = [
        pltpu.make_async_copy(source, target, semaphores.at[number])
        for number, (source, target) in enumerate(moves)
    ]
    for copy in copies:
        copy.start()
    for copy in copies[:4]:
        copy.wait()
    positions = numbers[...].astype(jnp.float32)
    out[starts["places"] : starts["places"] + 8, :] = jnp.concatenate([positions, positions], axis=0)
    for name, ref in (("f0", s0), ("f1", s1), ("f2", s2)):
        rows, width = ref.shape
        for chunk in range(width // LANES):
            at = starts[name] + chunk * rows
            out[at : at + rows, :] = ref[:, chunk * LANES : (chunk + 1) * LANES]
    for copy in copies[4:]:
        copy.wait()
    tail[...] = out[part[0] : part[1], :]


def own_targets(sizes, owned, taken):
    device_index = lax.axis_index("gx") * lax.axis_size("gy") + lax.axis_index("gy")
    columns = lax.broadcasted_iota(jnp.int32, (1, sum(owned)), 1)
    target = columns
    before = 0
    level_start = 0
    for section in range(4):
        rank = jnp.int32(0)
        for bit_number in sorted(taken[section], reverse=True):
            rank = rank * 2 + ((device_index >> bit_number) & 1)
        here = columns - before + (level_start + rank * owned[section])
        target = jnp.where(columns >= before, here, target)
        before += owned[section]
        level_start += sizes[section]
    return target


def forward_body(sizes, owned, taken, rhs, inverse, lower, sep_rhs, places, coupling, forward, sums):
    count, block = inverse.shape[2], inverse.shape[3]
    alone, steps = [], [None]
    for counter in range(count):
        pieces = halves(inverse[0, 0, counter])
        alone.append(times(rhs[0, 0, :, counter * block : (counter + 1) * block], pieces, False))
        if counter > 0:
            steps.append(halves(times(lower[0, 0, counter - 1], pieces, False)))
    earlier = None
    for counter in range(count):
        current = alone[counter]
        if counter > 0:
            current = current - times(earlier, steps[counter], False)
        earlier = current
        forward[:, counter * block : (counter + 1) * block] = earlier
    whole = forward[...]
    own = times(sep_rhs[0, 0], [one_hot(own_targets(sizes, owned, taken), sum(sizes))], True)
    terms = times(whole, halves(coupling[0, 0].reshape(-1, whole.shape[1])), True)
    width = coupling.shape[3]
    at = 0
    for section in range(4):
        term = terms[:, section * width : (section + 1) * width]
        spread = times(term, [one_hot(places[0, 0, section : section + 1, :], sizes[section])], True)
        sums[:, at : at + sizes[section]] = own[:, at : at + sizes[section]] - spread
        at += sizes[section]


def gather_body(section, starts, rows, size, above, places, *refs):
    outs = refs[len(places) :]
    at = 0
    for ref, bases in zip(refs, places):
        for base in bases:
            factor = wide(ref, base + starts["f%d" % section], rows, size // LANES)
            outs[0][at : at + rows, :], outs[1][at : at + rows, :] = halves(factor)
            if section > 0:
                place = base + starts["l%d" % section]
                link = ref[place : place + rows, :]
                row = base + starts["places"] + section - 1
                positions = ref[row : row + 1, :].astype(jnp.int32)
                linked = times(link, [one_hot(positions, above)], True)
                outs[2][at : at + rows, :], outs[3][at : at + rows, :] = halves(linked)
            at += rows


def eliminate_body(size, above, tables, mine, theirs, *refs):
    sums, found = refs[4 * tables :]
    width = mine.shape[1]
    total = mine[...] + theirs[...]
    right_side = total[:, width - size :]
    rest = total[:, width - size - above : width - size]
    at = 0
    for table in range(tables):
        f_high, f_low, m_high, m_low = refs[4 * table : 4 * table + 4]
        solved = times(right_side, [f_high[...], f_low[...]], True)
        found[:, at : at + solved.shape[1]] = solved
        rest = rest - times(solved, [m_high[...], m_low[...]], False)
        at += solved.shape[1]
    if width > size + above:
        sums[:, : width - size - above] = total[:, : width - size - above]
    sums[:, width - size - above :] = rest


def top_body(total, f_high, f_low, partial):
    pieces = [f_high[...], f_low[...]]
    partial[...] = times(times(total[...], pieces, True), pieces, False)


def last_top_body(total, earlier, f_high, f_low, partial):
    pieces = [f_high[...], f_low[...]]
    partial[...] = earlier[...] + times(times(total[...], pieces, True), pieces, False)


def join_body(moves, *refs):
    for number, start, at, rows in moves:
        refs[-1][at : at + rows, :] = refs[number][start : start + rows, :]


def copy_body(arrived, out):
    out[...] = arrived[...]


def add_body(mine, theirs, out):
    out[...] = mine[...] + theirs[...]


def fold_body(tables, found, *refs):
    solved, n_high, n_low = refs[4 * tables :]
    dims = (((0,), (0,)), ((), ()))
    known = folded = None
    at = 0
    for table in range(tables):
        f_high, f_low, m_high, m_low = refs[4 * table : 4 * table + 4]
        rows = f_high.shape[0]
        pieces = [f_high[...], f_low[...]]
        term = times(found[:, at : at + rows], pieces, False)
        known = term if known is None else known + term
        for link in (m_high[...], m_low[...]):
            for piece in pieces:
                term = lax.dot_general(link, piece, dims, preferred_element_type=jnp.float32)
                folded = term if folded is None else folded + term
        at += rows
    solved[...] = known
    n_high[...], n_low[...] = halves(folded)


def leaf_body(sections, forward, coupling, inverse, lower, *outs):
    count, block = inverse.shape[2], inverse.shape[3]
    d_high, d_low = outs[-2:]
    rows = [coupling[0, 0, section] for section in sections]
    if len(outs) == 3:
        rows = [forward[...]] + rows
    rows = jnp.concatenate(rows, axis=0)
    first = rows.shape[0] - d_high.shape[0]
    later = None
    for counter in reversed(range(count)):
        current = rows[:, counter * block : (counter + 1) * block]
        if counter < count - 1:
            current = current - wide_times(later, lower[0, 0, counter])
        later = wide_times(current, inverse[0, 0, counter])
        columns = slice(counter * block, (counter + 1) * block)
        if first:
            outs[0][:, columns] = later[:first]
        d_high[:, columns], d_low[:, columns] = halves(later[first:])


def pick_body(sizes, owned, taken, places, picks, owns):
    at = 0
    for section in range(4):
        picks[at : at + sizes[section], :] = one_hot(places[0, 0, section : section + 1, :], sizes[section])
        at += sizes[section]
    owns[...] = one_hot(own_targets(sizes, owned, taken), at)


def backward_body(
    sizes, mine, theirs, u1, n1h, n1l, u2, n2h, n2l, u3, n3h, n3l, base, d1h, d1l, d2h, d2l, picks, owns, leaf, sep
):
    starts = [sum(sizes[:section]) for section in range(4)]

    def pick(section):
        return times(solved[section], [picks[starts[section] : starts[section] + sizes[section], :]], False)

    solved = [mine[...] + theirs[...]]
    solved.append(u1[...] - times(solved[0], [n1h[...], n1l[...]], False))
    picked = [pick(0)]
    solved.append(u2[...] - times(solved[1], [n2h[...], n2l[...]], False))
    picked.append(pick(1))
    solved.append(u3[...] - times(solved[2], [n3h[...], n3l[...]], False))
    first = base[...] - times(jnp.concatenate(picked, axis=1), [d1h[...], d1l[...]], False)
    owned = times(jnp.concatenate(solved[:3], axis=1), [owns[: starts[3], :]], False)
    picked = jnp.concatenate([pick(2), pick(3)], axis=1)
    leaf[0, 0] = first - times(picked, [d2h[...], d2l[...]], False)
    sep[0, 0] = owned + times(solved[3], [owns[starts[3] :, :]], False)


def gathered(
    rhs_leaf,
    leaf_inv,
    leaf_sub,
    sep_rhs,
    interface,
    coupling,
    factor_one,
    factor_two,
    factor_three,
    factor_four,
    link_two,
    link_three,
    link_four,
):
    gy_bits = lax.axis_size("gy").bit_length() - 1
    gx_bits = lax.axis_size("gx").bit_length() - 1
    taken = taken_lists(gy_bits, gx_bits)
    factors = [array.reshape(array.shape[2:]) for array in (factor_one, factor_two, factor_three, factor_four)]
    links = [array.reshape(array.shape[2:]) for array in (link_two, link_three, link_four)]
    sizes = tuple(factor.shape[1] for factor in factors)
    owned = tuple(factor.shape[0] for factor in factors)
    starts, sets, height = packed_layout(factors, links)
    axes = ("gx", "gy")
    core = gy_bits
    rhs_count = rhs_leaf.shape[2]
    total = sum(sizes)

    part = (sets[1][0], sets[2][1])
    packed, tail = vmem_call(
        functools.partial(pack_body, starts, part),
        [((height, LANES), jnp.float32), ((part[1] - part[0], LANES), jnp.float32)],
        factor_one, factor_two, factor_three, factor_four, link_two, link_three, link_four, interface,
        microseconds=1.0, space=pltpu.HBM,
        scratch=[pltpu.VMEM(factor.shape, jnp.float32) for factor in factors[:3]]
        + [pltpu.VMEM(interface.shape[2:], jnp.int32), pltpu.SemaphoreType.DMA((8,))],
    )

    everything = (0, 1, 2, 3)
    whole = ((0, everything),)
    both = [(packed, whole), (from_partner(packed, axes, core), whole)]

    def plan(wanted):
        moves, members, at = [], [], 0
        for number, (_, have) in enumerate(wanted):
            for base, its_sets, travels in have:
                first, last = sets[travels[0]][0], sets[travels[-1]][1]
                moves.append((number, base + first, at, last - first))
                members.append((at - first, travels))
                at += last - first
        return tuple(moves), tuple(members), at

    def choose(buffers, *travels):
        wanted = []
        for array, members in buffers:
            have = []
            for base, its_sets in members:
                fit = [run for run in travels if set(run) <= set(its_sets)]
                if fit:
                    have.append((base, its_sets, fit[0]))
            if have:
                wanted.append((array, tuple(have)))
        return wanted

    def message(wanted, after, microseconds=ARRIVE_US):
        moves, members, rows = plan(wanted)
        (out,) = vmem_call(
            functools.partial(join_body, moves), [((rows, LANES), jnp.float32)],
            *[array for array, _ in wanted], after=after, microseconds=microseconds,
        )
        return out, members

    def arrive(arrived, members, after, microseconds=ARRIVE_US):
        (copy,) = vmem_call(
            copy_body, [(arrived.shape, jnp.float32)], arrived, after=after, microseconds=microseconds
        )
        both.extend([(copy, members), (from_partner(copy, axes, core), members)])
        return copy, members

    def level(section, buffers, after=()):
        rows, size = factors[section].shape
        above = sizes[section - 1] if section > 0 else 0
        chosen = choose(buffers, (section,))
        places = tuple(tuple(base for base, _, _ in have) for _, have in chosen)
        count = sum(len(bases) for bases in places)
        outs = [((count * rows, size), jnp.bfloat16)] * 2
        if section > 0:
            outs = outs + [((count * rows, above), jnp.bfloat16)] * 2
        body = functools.partial(gather_body, section, starts, rows, size, above, places)
        return vmem_call(body, outs, *[array for array, _ in chosen], microseconds=TABLE_US, after=after)

    def eliminate(section, sums, theirs, tables, after):
        size, above = sizes[section], sizes[section - 1]
        flat = [array for table in tables for array in table]
        sums, found = vmem_call(
            functools.partial(eliminate_body, size, above, len(tables)),
            [((rhs_count, sums.shape[1] - size), jnp.float32), ((rhs_count, size), jnp.float32)],
            sums, theirs, *flat, microseconds=ELIM_US, after=after,
        )
        return sums, (found, *flat)

    def fold(section, pieces, after):
        size, above = sizes[section], sizes[section - 1]
        return vmem_call(
            functools.partial(fold_body, (len(pieces) - 1) // 4),
            [((rhs_count, size), jnp.float32)] + [((above, size), jnp.bfloat16)] * 2,
            *pieces, microseconds=FOLD_US, after=after,
        )

    def solve(sections, with_forward, after):
        rows = len(sections) * LANES
        return vmem_call(
            functools.partial(leaf_body, sections),
            [((rhs_count, rhs_leaf.shape[3]), jnp.float32)] * with_forward
            + [((rows, rhs_leaf.shape[3]), jnp.bfloat16)] * 2,
            forward, coupling, leaf_inv, leaf_sub, microseconds=LEAF_US, after=after,
        )

    inner = min(taken[3]) if core == max(taken[3]) else max(taken[3])
    third, second, first = gy_bits + gx_bits - 2, gy_bits - 1, gy_bits + gx_bits - 1

    from_inner = from_partner(packed, axes, inner)
    from_third = from_partner(tail, axes, third)
    forward, sums = vmem_call(
        functools.partial(forward_body, sizes, owned, taken),
        [((rhs_count, rhs_leaf.shape[3]), jnp.float32), ((rhs_count, total), jnp.float32)],
        rhs_leaf, leaf_inv, leaf_sub, sep_rhs, interface, coupling, microseconds=SOLVE_US,
    )
    others = from_partner(sums, axes, core)
    by_third = arrive(from_third, ((-part[0], (1, 2)),), ())
    (sums,) = vmem_call(
        add_body, [((rhs_count, total), jnp.float32)], sums, others, microseconds=0.1, after=(by_third[0],)
    )
    theirs = from_partner(sums, axes, inner)
    by_inner = arrive(from_inner, whole, (sums,))
    following, two_at = message(choose([by_third], (1, 2)), (sums,))
    two = from_partner(following, axes, inner)
    following, near_at = message(choose([both[0], by_inner], (0, 1)), (sums,))
    near = from_partner(following, axes, second)
    table = level(3, both)
    sums, four_level = eliminate(3, sums, theirs, [table], ())

    theirs = from_partner(sums, axes, third)
    solved_first = solve((0, 1), True, (sums,))
    by_two = arrive(two, two_at, (solved_first[0],), X2_US)
    following, last_at = message(choose([by_third, by_two], (1,)), (sums,), Y2_US)
    by_near = arrive(near, near_at, (following,), NEAR_US)
    last = from_partner(following, axes, second)
    table = level(2, both)
    sums, three_level = eliminate(2, sums, theirs, [table], ())

    theirs = from_partner(sums, axes, second)
    following, top_at = message(choose([both[0], by_inner, by_near], (0,)), (sums,), F1_US)
    from_third = from_partner(following, axes, third)
    early = len(both)
    table = level(1, both[:early], (sums,))
    arrive(last, last_at, (table[0],), LAST_US)
    folded_three = fold(2, three_level, (sums,))
    late = (folded_three[0],)
    sums, two_level = eliminate(1, sums, theirs, [table, level(1, both[early:])], late)

    theirs = from_partner(sums, axes, first)
    folded_two = fold(1, two_level, (sums,))
    arrive(from_third, top_at, (sums,), F1C_US)
    table = level(0, both[:-2], (sums,))
    (sums,) = vmem_call(
        add_body, [((rhs_count, sizes[0]), jnp.float32)], sums, theirs, microseconds=SUM_US,
        after=(folded_two[0], table[0]),
    )
    (near_part,) = vmem_call(
        top_body, [((rhs_count, sizes[0]), jnp.float32)], sums, *table, microseconds=0.4
    )
    (partial,) = vmem_call(
        last_top_body, [((rhs_count, sizes[0]), jnp.float32)],
        sums, near_part, *level(0, both[-2:], (near_part,)), microseconds=0.4,
    )
    theirs = from_partner(partial, axes, first)
    solved_second = solve((2, 3), False, (partial,))
    folded_four = fold(3, four_level, (partial,))
    picks = vmem_call(
        functools.partial(pick_body, sizes, owned, taken),
        [((total, interface.shape[3]), jnp.bfloat16), ((total, sum(owned)), jnp.bfloat16)],
        interface, microseconds=0.3, after=(partial,),
    )
    leaf, sep = vmem_call(
        functools.partial(backward_body, sizes),
        [(rhs_leaf.shape, jnp.float32), (sep_rhs.shape, jnp.float32)],
        partial, theirs, *folded_two, *folded_three, *folded_four, *solved_first, *solved_second, *picks,
        microseconds=2.0,
    )
    return (leaf, sep)


def local(*arrays):
    gathered_bytes = 0
    bits = lax.axis_size("gy").bit_length() + lax.axis_size("gx").bit_length() - 2
    for level, array in enumerate(arrays[6:10]):
        gathered_bytes += array.size * 4 << (bits - level)
    gy_bits = lax.axis_size("gy").bit_length() - 1
    fourth = taken_lists(gy_bits, bits - gy_bits)[3]
    if gathered_bytes > GATHER_BYTES or len(fourth) != 2 or gy_bits not in fourth:
        return level_by_level(*arrays)
    return gathered(*arrays)


def solution(mesh):
    in_specs = (
        P("gx", "gy", None, None),
        P("gx", "gy", None, None, None),
        P("gx", "gy", None, None, None),
        P("gx", "gy", None, None),
        P("gx", "gy", None, None),
        P("gx", "gy", None, None, None),
        P("gx", "gy", None, None),
        P("gx", "gy", None, None),
        P("gx", "gy", None, None),
        P("gx", "gy", None, None),
        P("gx", "gy", None, None),
        P("gx", "gy", None, None),
        P("gx", "gy", None, None),
    )
    out_specs = (P("gx", "gy", None, None), P("gx", "gy", None, None))
    return jax.shard_map(local, mesh=mesh, in_specs=in_specs, out_specs=out_specs, check_vma=False)
```
